128 devices in a mesh: lon: 32 (over x, z, core), bin: 4 (over y).
Axes of the slice: x: 4, y: 4, z: 4, core: 2. Of those that a mesh axis runs over, the one named last changes fastest.
Arguments:
- spectrum: float32 [1296, 1440, 128], P('bin', 'lon'), may hold values from 0.05 to 1
- sea_mask: int32 [1440, 128], P('lon'), may hold values from 0 to 1, as said below
- cour_lon: float32 [1296, 128], P('bin'), may hold values from -0.45 to 0.45
- cour_lat: float32 [1296], P('bin'), may hold values from -0.45 to 0.45
- wind: float32 [1440, 128], P('lon'), may hold values from 0.5 to 2
- growth_rate: float32 [1296], replicated, may hold values from 0.05 to 0.5
- band_weight: float32 [1296], replicated, may hold values from 0.00038580247 to 0.0030864198
- freq_mix: float32 [36, 36], replicated, may hold values from -1 to 1
- dir_mix: float32 [36, 36], replicated, may hold values from -1 to 1
- routes: int32 [32, 128, 32], P('lon'), may hold values from 0 to 5759, as said below
- counts: int32 [32, 128], P('lon'), may hold values from 0 to 32, as said below
Outputs:
- new_spectrum: float32 [1296, 1440, 128], P('bin', 'lon')
The draws below stay inside these ranges and needn't reach their ends.
Inputs may be any that keep to these rules, and one draw needn't show every extreme that they name: `routes`: for block g and owner o, entries s < counts[g, o] name distinct cells of block g; together they name every sea cell of the block once; unused entries are 0. `counts`: in every draw one owner gets 32 cells from every block. `sea_mask`: 1 exactly at the cells named by routes; a block holds from 2048 to 4096 sea cells, some block exactly the latter.
All inputs are finite; a program needn't handle non-finite values.
Results may differ from the reference program's by a relative error of at most 0.0001.
Values sent between devices are 32-bit elements; how exact they have to be, the bound alone decides.
A program may use at most 128 MiB of HBM per device.

```python
import math
import jax
import jax.numpy as jnp
from jax import lax

NF = 36
ND = 36
CLON = 45
NLAT = 128
K = 1296
BLOCKS = 32
NLON = 1440
OWNERS = 128
CAP = 32


def arrange(key):
    cells = CLON * NLAT
    most = OWNERS * CAP
    key_order, key_total, key_full, key_owner = jax.random.split(key, 4)
    orders = jax.vmap(lambda each: jax.random.permutation(each, cells))(jax.random.split(key_order, BLOCKS)).astype(jnp.int32)
    totals = jax.random.randint(key_total, (BLOCKS,), most // 2, most + 1)
    totals = totals.at[jax.random.randint(key_full, (), 0, BLOCKS)].set(most)
    chosen = jax.random.randint(key_owner, (), 0, OWNERS)
    owner = jnp.arange(OWNERS)[:, None]
    place_slot = jnp.arange(CAP)[None, :]
    spread = (owner - chosen - 1) % OWNERS
    place = jnp.where(owner == chosen, place_slot, CAP + place_slot * (OWNERS - 1) + spread)
    valid = place[None, :, :] < totals[:, None, None]
    named = orders[:, jnp.minimum(place, cells - 1)]
    routes = jnp.where(valid, named, 0).astype(jnp.int32)
    counts = jnp.sum(valid.astype(jnp.int32), axis=2).astype(jnp.int32)
    flags = (jnp.arange(cells)[None, :] < totals[:, None]).astype(jnp.int32)
    rows_index = jnp.arange(BLOCKS)[:, None]
    sea = jnp.zeros((BLOCKS, cells), jnp.int32).at[rows_index, orders].set(flags)
    return (routes, counts, sea.reshape(NLON, NLAT))


def draw_routes(key, part):
    tables = arrange(key)
    return tables[0]


def draw_counts(key, part):
    tables = arrange(key)
    return tables[1]


def draw_sea_mask(key, part):
    tables = arrange(key)
    return tables[2]


def block_scale(own_key, shape, cuts, least, high):
    level = 1.0
    for axis_at, blocks in cuts:
        draws = jax.random.uniform(jax.random.fold_in(jax.random.fold_in(own_key, 6), axis_at), (blocks,), jnp.float32, least / len(cuts), high / len(cuts))
        level = level * jnp.repeat(jnp.exp(draws), shape[axis_at] // blocks).reshape((-1,) + (1,) * (len(shape) - 1 - axis_at))
    return level


def scatter_about(key, dims, scale, limit, kind=jnp.bfloat16):
    entries = scale * jax.random.normal(key, dims, jnp.float32)
    return jnp.clip(entries, min=-limit, max=limit).astype(kind)


def setup_inputs(seed: int = 0) -> dict:
    key_of = jax.random.split(jax.random.key(seed), 12)
    return {
        "spectrum": jnp.clip(jnp.exp(math.log(1.0) - 2.9957323 * jax.random.uniform(key_of[0], (K, NLON, NLAT), jnp.float32) ** block_scale(key_of[0], (K, NLON, NLAT), ((0, 4), (1, 32)), -0.2, 0.2)), 0.05, 1.0),
        "sea_mask": draw_sea_mask(jax.random.fold_in(key_of[11], 71), 0),
        "cour_lon": jnp.clip(jax.random.uniform(key_of[2], (K, NLAT), jnp.float32, -0.45, 0.45) * block_scale(key_of[2], (K, NLAT), ((0, 4),), -0.4, 0.0), -0.45, 0.45),
        "cour_lat": jnp.clip(jax.random.uniform(key_of[3], (K,), jnp.float32, -0.45, 0.45) * block_scale(key_of[3], (K,), ((0, 4),), -0.4, 0.0), -0.45, 0.45),
        "wind": jnp.clip(jnp.exp(math.log(2.0) - 1.3862944 * jax.random.uniform(key_of[4], (NLON, NLAT), jnp.float32) ** block_scale(key_of[4], (NLON, NLAT), ((0, 32),), -0.2, 0.2)), 0.5, 2.0),
        "growth_rate": jnp.clip(jnp.exp(jax.random.uniform(key_of[5], (K,), jnp.float32, math.log(0.05), math.log(0.5))), 0.05, 0.5),
        "band_weight": jnp.clip(jnp.exp(jax.random.uniform(key_of[6], (K,), jnp.float32, math.log(0.00038580247), math.log(0.0030864198))), 0.00038580247, 0.0030864198),
        "freq_mix": scatter_about(key_of[7], (NF, NF), NF ** -0.5, 1.0, jnp.float32),
        "dir_mix": scatter_about(key_of[8], (ND, ND), ND ** -0.5, 1.0, jnp.float32),
        "routes": draw_routes(jax.random.fold_in(key_of[11], 71), 0),
        "counts": draw_counts(jax.random.fold_in(key_of[11], 71), 0),
    }


dissipation = 0.5
time_step = 0.5


def advect(padded, cour_lon, cour_lat):
    middle = padded[:, 1:-1, :]
    west = padded[:, :-2, :]
    east = padded[:, 2:, :]
    zero = jnp.zeros_like(middle[:, :, :1])
    south = jnp.concatenate([zero, middle[:, :, :-1]], axis=2)
    north = jnp.concatenate([middle[:, :, 1:], zero], axis=2)
    along = cour_lon[:, None, :]
    across = cour_lat[:, None, None]
    return (middle - jnp.maximum(along, 0.0) * (middle - west) - jnp.minimum(along, 0.0) * (east - middle)
            - jnp.maximum(across, 0.0) * (middle - south) - jnp.minimum(across, 0.0) * (north - middle))


def sources(full, speed, growth_rate, band_weight, freq_mix, dir_mix):
    steep = jnp.sum(band_weight[:, None] * full, axis=0)
    factor = growth_rate[:, None] * speed[None, :] - dissipation * steep / (1.0 + steep)
    cube = full.reshape(freq_mix.shape[0], dir_mix.shape[0], full.shape[1])
    mixed = jnp.einsum('fg,gdm->fdm', freq_mix, cube, precision=lax.Precision.HIGHEST)
    mixed = jnp.einsum('de,fem->fdm', dir_mix, mixed, precision=lax.Precision.HIGHEST)
    return full * factor + mixed.reshape(full.shape)


def reference(spectrum, sea_mask, cour_lon, cour_lat, wind, growth_rate, band_weight, freq_mix, dir_mix, routes, counts):
    cells = CLON * NLAT
    valid = jnp.arange(CAP)[None, None, :] < counts[:, :, None]
    offsets = (jnp.arange(BLOCKS) * cells).astype(jnp.int32)[:, None, None]
    places = (routes + offsets).reshape(-1)
    active = jnp.zeros((NLON * NLAT,), jnp.float32).at[places].add(valid.reshape(-1).astype(jnp.float32))
    active = active.reshape(NLON, NLAT)
    sea = sea_mask.astype(jnp.float32)

    def one_block(block, result):
        first = (block * CLON).astype(jnp.int32)
        columns = (first - 1 + jnp.arange(CLON + 2).astype(jnp.int32)) % NLON
        sea_wide = jnp.take(sea, columns, axis=0)
        padded = jnp.take(spectrum, columns, axis=1) * sea_wide[None]
        moved = advect(padded, cour_lon, cour_lat) * sea_wide[None, 1:-1, :]
        flat = moved.reshape(K, cells)
        zero = jnp.int32(0)
        live = lax.dynamic_slice(active, (first, zero), (CLON, NLAT)).reshape(cells)
        speed = lax.dynamic_slice(wind, (first, zero), (CLON, NLAT)).reshape(cells)
        source = sources(flat, speed, growth_rate, band_weight, freq_mix, dir_mix)
        updated = (flat + time_step * (source * live[None, :])).reshape(K, CLON, NLAT)
        return lax.dynamic_update_slice(result, updated, (zero, first, zero))

    start = jnp.zeros((K, NLON, NLAT), jnp.float32)
    return lax.fori_loop(jnp.int32(0), jnp.int32(BLOCKS), one_block, start)
```

```python
import functools

import jax
import jax.numpy as jnp
import numpy as np
from jax import lax
from jax.experimental import pallas as pl
from jax.experimental.pallas import tpu as pltpu
from jax.sharding import PartitionSpec as P

MESH = pl.DeviceIdType.MESH
NF, ND = 36, 36
LON, LAT = 45, 128
GROUPS = 4
LOCAL = 324
PADDED = 328
CELLS = 4096
SHARE = CELLS // GROUPS
TILES = CELLS // LAT
SIZES = (64, 64, 64, 64, 72)
STARTS = (0, 64, 128, 192, 256)
PARTS = len(SIZES)
KSTARTS = tuple(GROUPS * s for s in STARTS)
KTOTAL = GROUPS * PADDED
MROWS = 336
UNROLL = 6


def column_maps():
    freq = np.zeros((NF, KTOTAL), np.float32)
    direction = np.zeros((ND, KTOTAL), np.float32)
    at = 0
    for start, size in zip(STARTS, SIZES):
        for p in range(GROUPS):
            for b in range(start, start + size):
                if b < LOCAL:
                    k = p * LOCAL + b
                    freq[k // ND, at] = 1.0
                    direction[k % ND, at] = 1.0
                at += 1
    return freq, direction


def tables(sea_mask):
    sea = jnp.roll(sea_mask.astype(jnp.float32), -1, axis=0)
    lanes = jnp.arange(LAT)
    upto = (lanes[:, None] <= lanes[None, :]).astype(jnp.float32)
    rank = jnp.dot(sea, upto).astype(jnp.int32)
    number = rank[:, -1].astype(jnp.float32)
    steps = jnp.arange(LON + 1)
    before = (steps[:, None] > steps[None, :LON]).astype(jnp.float32)
    offset_all = jnp.sum(before * number[None, :], axis=1).astype(jnp.int32)
    offset = offset_all[:LON]
    shift = offset % LAT
    wanted = (lanes[None, :] - shift[:, None]) % LAT
    source = jnp.sum((rank[:, :, None] <= wanted[:, None, :]).astype(jnp.int32), axis=1)
    source = jnp.minimum(source, LAT - 1)
    low = (lanes[None, :] >= shift[:, None]).astype(jnp.int32)
    cross = jnp.broadcast_to((shift[:, None] + rank[:, -1:] >= LAT).astype(jnp.int32), (LON, LAT))
    ends = jnp.arange(TILES) * LAT + LAT - 1
    last = jnp.sum((offset_all[None, :] <= ends[:, None]).astype(jnp.int32), axis=1) - 1
    first = jnp.minimum(offset // LAT, TILES - 1)
    place = (shift[:, None] + rank - 1) % LAT

    def wide(a):
        return jnp.broadcast_to(a[:, None, :], (a.shape[0], 8, LAT))

    return wide(sea), wide(source), wide(low), wide(cross), last, first, wide(place)


def exchange_kernel(
    last_ref, spec_ref, coef_ref, sea_ref, source_ref, low_ref, cross_ref, fmix_ref, dmix_ref, fcol_ref, dcol_ref,
    moved_ref, mixed_ref, damp_ref,
    x, halo, sea_halo, packed, stage, recv_a, recv_b, acc, w_hi_a, w_lo_a, w_hi_b, w_lo_b, fcols, dcols,
    steep, sums,
    in_sem, out_sem, halo_send, halo_recv, send_sem, recv_sem, back_send, back_recv, sum_send, sum_recv, own_sem,
):
    me = lax.axis_index("bin")
    block = lax.axis_index("lon")
    blocks = lax.axis_size("lon")
    west = lax.rem(block + blocks - 1, blocks)
    east = lax.rem(block + 1, blocks)

    def peer(d):
        return lax.rem(me + d, GROUPS)

    loads = []
    for c in range(PARTS):
        rows = min(SIZES[c], LOCAL - STARTS[c])
        copy = pltpu.make_async_copy(
            spec_ref.at[:, pl.ds(STARTS[c], rows), :], x.at[:, pl.ds(STARTS[c], rows), :], in_sem.at[c]
        )
        copy.start()
        loads.append(copy)

    barrier = pltpu.get_barrier_semaphore()
    for d in (1, 2, 3):
        pl.semaphore_signal(barrier, inc=1, device_id=(block, peer(d)), device_id_type=MESH)
    pl.semaphore_signal(barrier, inc=1, device_id=(west, me), device_id_type=MESH)
    pl.semaphore_signal(barrier, inc=1, device_id=(east, me), device_id_type=MESH)
    pl.semaphore_wait(barrier, 5)

    edges = []
    for slot, row, step, to in ((0, LON - 1, LON - 2, east), (1, 0, LON - 1, west)):
        copy = pltpu.make_async_remote_copy(
            src_ref=spec_ref.at[row], dst_ref=halo.at[slot, pl.ds(0, LOCAL), :],
            send_sem=halo_send.at[slot], recv_sem=halo_recv.at[slot], device_id=(to, me), device_id_type=MESH,
        )
        copy.start()
        edges.append(copy)
        copy = pltpu.make_async_remote_copy(
            src_ref=sea_ref.at[step], dst_ref=sea_halo.at[slot],
            send_sem=halo_send.at[2 + slot], recv_sem=halo_recv.at[2 + slot], device_id=(to, me), device_id_type=MESH,
        )
        copy.start()
        edges.append(copy)

    steep[...] = jnp.zeros_like(steep)
    pad = PADDED - LOCAL
    x[:, pl.ds(LOCAL, pad), :] = jnp.zeros((LON, pad, LAT), jnp.float32)
    halo[:, pl.ds(LOCAL, pad), :] = jnp.zeros((2, pad, LAT), jnp.float32)

    def advect_rows(start, n, base):
        at = [pl.ds(pl.multiple_of(base + 8 * j, 8), 8) for j in range(n)]
        to = [pl.ds(pl.multiple_of(base - start + 8 * j, 8), 8) for j in range(n)]
        coef = [[coef_ref[q, at[j], :] for q in range(6)] for j in range(n)]

        def finish(i, row, low_side, mid, high_side, hold):
            sea = sea_ref[i]
            source = source_ref[i]
            low = low_ref[i] != 0
            cross = cross_ref[i] != 0
            total = steep[i]
            new_hold = []
            for j in range(n):
                c0, cw, ce, cs, cn, weight = coef[j]
                m = mid[j]
                value = c0 * m + cw * low_side[j] + ce * high_side[j]
                value = value + cs * pltpu.roll(m, 1, 1) + cn * pltpu.roll(m, LAT - 1, 1)
                value = value * sea
                x[row, at[j], :] = value
                total = total + weight * value
                turned = jnp.take_along_axis(value, source, axis=1)
                kept = jnp.where(low, turned, hold[j])
                packed[i, to[j], :] = kept
                new_hold.append(jnp.where(cross, turned, kept))
            steep[i] = total
            return tuple(new_hold)

        first = tuple(x[0, at[j], :] * sea_ref[LON - 1] for j in range(n))
        second = tuple(x[1, at[j], :] * sea_ref[0] for j in range(n))
        zero = tuple(jnp.zeros((8, LAT), jnp.float32) for j in range(n))

        def one(i, carry):
            low_side, mid, hold = carry
            sea_next = sea_ref[i + 1]
            high_side = tuple(x[i + 2, at[j], :] * sea_next for j in range(n))
            hold = finish(i, i + 1, low_side, mid, high_side, hold)
            return (mid, high_side, hold)

        def several(s, carry):
            for u in range(UNROLL):
                carry = one(s * UNROLL + u, carry)
            return carry

        carry = (first, second, zero)
        carry = lax.fori_loop(0, (LON - 3) // UNROLL, several, carry)
        carry = one(LON - 3, carry)
        low_side, mid, hold = carry
        high_side = tuple(halo[1, at[j], :] * sea_halo[1] for j in range(n))
        hold = finish(LON - 2, LON - 1, low_side, mid, high_side, hold)
        low_side = tuple(halo[0, at[j], :] * sea_halo[0] for j in range(n))
        hold = finish(LON - 1, 0, low_side, first, second, hold)
        for j in range(n):
            packed[LON, to[j], :] = hold[j]

    sends = []
    stores = []
    for c in range(PARTS):
        start, size = STARTS[c], SIZES[c]
        n = 2 if size % 16 == 0 else 3
        loads[c].wait()
        if c == 0:
            for copy in edges:
                copy.wait()

        def group(s, _, start=start, n=n):
            advect_rows(start, n, start + s * 8 * n)
            return 0

        lax.fori_loop(0, size // (8 * n), group, 0)
        rows = min(size, LOCAL - start)
        copy = pltpu.make_async_copy(
            x.at[:, pl.ds(start, rows), :], moved_ref.at[:, pl.ds(start, rows), :], out_sem.at[c]
        )
        copy.start()
        stores.append(copy)
        recv = recv_b if c == PARTS - 1 else recv_a.at[c]
        mine = pl.ds(pl.multiple_of(me * size, 8), size)
        for d in (2, 1, 3, 0):
            to = peer(d)
            for k in range(SHARE // LAT):
                row = last_ref[to * (SHARE // LAT) + k]
                value = packed[row, pl.ds(0, size), :]
                lanes = pl.ds(k * LAT, LAT)
                if d == 0:
                    recv[mine, lanes] = value
                else:
                    stage[d - 1, pl.ds(start, size), lanes] = value
            if d:
                copy = pltpu.make_async_remote_copy(
                    src_ref=stage.at[d - 1, pl.ds(start, size), :], dst_ref=recv.at[mine, :],
                    send_sem=send_sem.at[c, d - 1], recv_sem=recv_sem.at[c, d - 1],
                    device_id=(block, to), device_id_type=MESH,
                )
                copy.start()
                sends.append((c, copy))

    sums[0] = jnp.sum(steep[...], axis=1)
    sum_copies = []
    for d in (1, 2, 3):
        copy = pltpu.make_async_remote_copy(
            src_ref=sums.at[0], dst_ref=sums.at[d], send_sem=sum_send.at[d - 1], recv_sem=sum_recv.at[d - 1],
            device_id=(block, peer(d)), device_id_type=MESH,
        )
        copy.start()
        sum_copies.append(copy)

    exact = functools.partial(jnp.dot, precision=lax.Precision.HIGHEST, preferred_element_type=jnp.float32)
    fcols[...] = exact(fmix_ref[...], fcol_ref[...])
    spread = exact(dmix_ref[...], dcol_ref[...])
    for j in range(4):
        dcols[pl.ds(j * ND, ND), :] = spread

    def matrix_rows(p, _):
        for g, (size, count) in enumerate(((144, 4), (144, 4), (48, 1))):
            for c in range(PARTS):
                width = GROUPS * SIZES[c]
                cols = pl.ds(KSTARTS[c], width)
                index = lax.broadcasted_iota(jnp.int32, (size, width), 0)
                rows = [fcols[pl.ds(p * 9 + 4 * g + j, 1), cols] for j in range(count)]
                if count == 1:
                    factor = jnp.where(index < ND, rows[0], 0.0)
                else:
                    factor = jnp.where(
                        index < 2 * ND,
                        jnp.where(index < ND, rows[0], rows[1]),
                        jnp.where(index < 3 * ND, rows[2], rows[3]),
                    )
                value = factor * dcols[pl.ds(0, size), cols]
                high = value.astype(jnp.bfloat16)
                low = (value - high.astype(jnp.float32)).astype(jnp.bfloat16)
                at = pl.ds(144 * g, size)
                if c == PARTS - 1:
                    w_hi_b[p, at, :] = high
                    w_lo_b[p, at, :] = low
                else:
                    w_hi_a[c, p, at, :] = high
                    w_lo_a[c, p, at, :] = low
        return 0

    lax.fori_loop(0, GROUPS, matrix_rows, 0)

    dot = functools.partial(jnp.dot, preferred_element_type=jnp.float32)

    def halves(value):
        high = value.astype(jnp.bfloat16)
        return high, (value - high.astype(jnp.float32)).astype(jnp.bfloat16)

    for c in range(PARTS - 1):
        for at, copy in sends:
            if at == c:
                copy.wait_recv()

        def columns(s, _, c=c):
            lanes = pl.ds(pl.multiple_of(s * 256, 256), 256)
            high, low = halves(recv_a[c, :, lanes])

            def rows(p, _):
                value = dot(w_hi_a[c, p], high) + dot(w_lo_a[c, p], high) + dot(w_hi_a[c, p], low)
                if c:
                    value = value + acc[p, :, lanes]
                acc[p, :, lanes] = value
                return 0

            return lax.fori_loop(0, GROUPS, rows, 0)

        lax.fori_loop(0, SHARE // 256, columns, 0)

    for at, copy in sends:
        if at == PARTS - 1:
            copy.wait_recv()
    backs = []
    own = None
    lanes_here = pl.ds(pl.multiple_of(me * SHARE, SHARE), SHARE)
    for d in (2, 1, 3, 0):
        p = peer(d)

        def columns(s, _, p=p):
            lanes = pl.ds(pl.multiple_of(s * 256, 256), 256)
            high, low = halves(recv_b[:, lanes])
            value = dot(w_hi_b[p], high) + dot(w_lo_b[p], high) + dot(w_hi_b[p], low)
            acc[p, :, lanes] = value + acc[p, :, lanes]
            return 0

        lax.fori_loop(0, SHARE // 256, columns, 0)
        if d:
            copy = pltpu.make_async_remote_copy(
                src_ref=acc.at[p, pl.ds(0, PADDED), :], dst_ref=mixed_ref.at[:, lanes_here],
                send_sem=back_send.at[d - 1], recv_sem=back_recv.at[d - 1],
                device_id=(block, p), device_id_type=MESH,
            )
            copy.start()
            backs.append(copy)
        else:
            own = pltpu.make_async_copy(acc.at[p, pl.ds(0, PADDED), :], mixed_ref.at[:, lanes_here], own_sem)
            own.start()

    for copy in sum_copies:
        copy.wait()
    whole = (sums[0] + sums[1]) + (sums[2] + sums[3])
    damp_ref[...] = 0.5 * whole / (1.0 + whole)
    for copy in stores:
        copy.wait()
    for _, copy in sends:
        copy.wait_send()
    own.wait()
    for copy in backs:
        copy.wait()


def finish_kernel(first_ref, moved_ref, mixed_ref, grow_ref, wind_ref, damp_ref, sea_ref, low_ref, place_ref, out_ref):
    tiles = moved_ref.shape[1] // 8

    def tile(j, _):
        at = pl.ds(pl.multiple_of(j * 8, 8), 8)
        grow = grow_ref[at, :]

        def one(i, row):
            first = first_ref[i]
            here = mixed_ref[at, pl.ds(pl.multiple_of(first * LAT, LAT), LAT)]
            after = jnp.minimum(first + 1, TILES - 1)
            there = mixed_ref[at, pl.ds(pl.multiple_of(after * LAT, LAT), LAT)]
            joined = jnp.where(low_ref[i] != 0, here, there)
            term = jnp.take_along_axis(joined, place_ref[i], axis=1)
            value = moved_ref[row, at, :]
            source = value * (grow * wind_ref[i] - damp_ref[i]) + term
            out_ref[row, at, :] = value + 0.5 * jnp.where(sea_ref[i] != 0.0, source, 0.0)

        def several(s, _):
            for u in range(4):
                i = s * 4 + u
                one(i, i + 1)
            return 0

        lax.fori_loop(0, (LON - 1) // 4, several, 0)
        one(LON - 1, 0)
        return 0

    lax.fori_loop(0, tiles, tile, 0)


def on_device(
    spectrum, sea_mask, cour_lon, cour_lat, wind, growth_rate, band_weight, freq_mix, dir_mix, routes, counts
):
    spec = jnp.transpose(spectrum, (1, 0, 2))
    sea, source, low, cross, last, first, place = tables(sea_mask)
    me = lax.axis_index("bin")
    own_weight = lax.dynamic_slice(band_weight, (me * LOCAL,), (LOCAL,))
    own_growth = lax.dynamic_slice(growth_rate, (me * LOCAL,), (LOCAL,))
    lanes = jnp.arange(LAT)[None, :]
    along_up = jnp.maximum(cour_lon, 0.0)
    along_down = jnp.minimum(cour_lon, 0.0)
    across_up = jnp.broadcast_to(jnp.maximum(cour_lat, 0.0)[:, None], cour_lon.shape)
    across_down = jnp.broadcast_to(jnp.minimum(cour_lat, 0.0)[:, None], cour_lon.shape)
    coef = jnp.stack([
        1.0 - along_up + along_down - across_up + across_down,
        along_up,
        -along_down,
        jnp.where(lanes == 0, 0.0, across_up),
        jnp.where(lanes == LAT - 1, 0.0, -across_down),
        jnp.broadcast_to(own_weight[:, None], cour_lon.shape),
    ])
    coef = jnp.pad(coef, ((0, 0), (0, PADDED - LOCAL), (0, 0)))
    fcol, dcol = column_maps()
    f32, bf16 = jnp.float32, jnp.bfloat16
    vmem = pl.BlockSpec(memory_space=pltpu.VMEM)
    hbm = pl.BlockSpec(memory_space=pl.ANY)
    smem = pl.BlockSpec(memory_space=pltpu.SMEM)
    dma = pltpu.SemaphoreType.DMA
    moved, mixed, damp = pl.pallas_call(
        exchange_kernel,
        out_shape=(
            jax.ShapeDtypeStruct((LON, LOCAL, LAT), f32),
            jax.ShapeDtypeStruct((PADDED, CELLS), f32),
            jax.ShapeDtypeStruct((LON, LAT), f32),
        ),
        in_specs=[smem, hbm] + [vmem] * 9,
        out_specs=(hbm, hbm, vmem),
        scratch_shapes=[
            pltpu.VMEM((LON, PADDED, LAT), f32),
            pltpu.VMEM((2, PADDED, LAT), f32),
            pltpu.VMEM((2, 8, LAT), f32),
            pltpu.VMEM((LON + 1, max(SIZES), LAT), f32),
            pltpu.VMEM((GROUPS - 1, PADDED, SHARE), f32),
            pltpu.VMEM((PARTS - 1, GROUPS * SIZES[0], SHARE), f32),
            pltpu.VMEM((GROUPS * SIZES[-1], SHARE), f32),
            pltpu.VMEM((GROUPS, MROWS, SHARE), f32),
            pltpu.VMEM((PARTS - 1, GROUPS, MROWS, GROUPS * SIZES[0]), bf16),
            pltpu.VMEM((PARTS - 1, GROUPS, MROWS, GROUPS * SIZES[0]), bf16),
            pltpu.VMEM((GROUPS, MROWS, GROUPS * SIZES[-1]), bf16),
            pltpu.VMEM((GROUPS, MROWS, GROUPS * SIZES[-1]), bf16),
            pltpu.VMEM((NF, KTOTAL), f32),
            pltpu.VMEM((4 * ND, KTOTAL), f32),
            pltpu.VMEM((LON, 8, LAT), f32),
            pltpu.VMEM((GROUPS, LON, LAT), f32),
            dma((PARTS,)), dma((PARTS,)), dma((4,)), dma((4,)), dma((PARTS, 3)), dma((PARTS, 3)),
            dma((3,)), dma((3,)), dma((3,)), dma((3,)), dma,
        ],
        compiler_params=pltpu.CompilerParams(
            collective_id=0, has_side_effects=True, vmem_limit_bytes=52 << 20
        ),
    )(last, spec, coef, sea, source, low, cross, freq_mix, dir_mix, jnp.asarray(fcol), jnp.asarray(dcol))

    def wide(a):
        return jnp.broadcast_to(jnp.roll(a, -1, axis=0)[:, None, :], (LON, 8, LAT))

    grow = jnp.broadcast_to(own_growth[:, None], (LOCAL, LAT))
    step = 56
    whole = pl.BlockSpec((LON, 8, LAT), lambda c: (0, 0, 0))
    damp_wide = jnp.broadcast_to(damp[:, None, :], (LON, 8, LAT))
    out = pl.pallas_call(
        finish_kernel,
        out_shape=jax.ShapeDtypeStruct((LON, LOCAL, LAT), f32),
        grid=(pl.cdiv(LOCAL, step),),
        in_specs=[
            smem,
            pl.BlockSpec((LON, step, LAT), lambda c: (0, c, 0)),
            pl.BlockSpec((step, CELLS), lambda c: (c, 0)),
            pl.BlockSpec((step, LAT), lambda c: (c, 0)),
            whole, whole, whole, whole, whole,
        ],
        out_specs=pl.BlockSpec((LON, step, LAT), lambda c: (0, c, 0)),
        compiler_params=pltpu.CompilerParams(vmem_limit_bytes=40 << 20),
    )(first, moved, mixed, grow, wide(wind), damp_wide, sea, low, place)
    return jnp.transpose(out, (1, 0, 2))


def solution(mesh):
    placed = (
        P("bin", "lon", None),
        P("lon", None),
        P("bin", None),
        P("bin"),
        P("lon", None),
        P(),
        P(),
        P(),
        P(),
        P("lon", None, None),
        P("lon", None),
    )
    return jax.shard_map(
        on_device, mesh=mesh, in_specs=placed, out_specs=P("bin", "lon", None), check_vma=False
    )
```

```python
import functools

import jax
import jax.numpy as jnp
import numpy as np
from jax import lax
from jax.experimental import pallas as pl
from jax.experimental.pallas import tpu as pltpu
from jax.sharding import PartitionSpec as P

MESH = pl.DeviceIdType.MESH
NF, ND = 36, 36
LON, LAT = 45, 128
GROUPS = 4
LOCAL = 324
PADDED = 328
CELLS = 4096
SHARE = CELLS // GROUPS
TILES = CELLS // LAT
SIZES = (64, 64, 64, 64, 72)
STARTS = (0, 64, 128, 192, 256)
PARTS = len(SIZES)
KSTARTS = tuple(GROUPS * s for s in STARTS)
KTOTAL = GROUPS * PADDED
MROWS = 336
ROWS_AT_ONCE = 10


def column_maps():
    freq = np.zeros((NF, KTOTAL), np.float32)
    direction = np.zeros((ND, KTOTAL), np.float32)
    at = 0
    for start, size in zip(STARTS, SIZES):
        for p in range(GROUPS):
            for b in range(start, start + size):
                if b < LOCAL:
                    k = p * LOCAL + b
                    freq[k // ND, at] = 1.0
                    direction[k % ND, at] = 1.0
                at += 1
    return freq, direction


def exchange_kernel(
    spec_ref, mask_ref, cour_ref, lat_ref, wind_ref, growth_ref, weight_ref, fmix_ref, dmix_ref, fcol_ref, dcol_ref,
    moved_ref, mixed_ref, damp_ref, gust_ref, live_ref, low_ref, place_ref, first_ref, grow_ref,
    x, moved, sea, source, cross, order, last_rows, last, coef, packed, stage, recv_a, recv_b, acc,
    w_hi_a, w_lo_a, w_hi_b, w_lo_b, fcols, dcols, steep, sums,
    in_sem, out_sem, halo_send, halo_recv, send_sem, recv_sem, back_send, back_recv, sum_send, sum_recv, own_sem, last_sem,
):
    me = lax.axis_index("bin")
    block = lax.axis_index("lon")
    blocks = lax.axis_size("lon")
    west = lax.rem(block + blocks - 1, blocks)
    east = lax.rem(block + 1, blocks)

    def peer(d):
        return lax.rem(me + d, GROUPS)

    barrier = pltpu.get_barrier_semaphore()
    for d in (1, 2, 3):
        pl.semaphore_signal(barrier, inc=1, device_id=(block, peer(d)), device_id_type=MESH)
    pl.semaphore_signal(barrier, inc=1, device_id=(west, me), device_id_type=MESH)
    pl.semaphore_signal(barrier, inc=1, device_id=(east, me), device_id_type=MESH)

    loads = []
    for c in range(PARTS):
        rows = min(SIZES[c], LOCAL - STARTS[c])
        copy = pltpu.make_async_copy(
            spec_ref.at[:, pl.ds(STARTS[c], rows), :],
            x.at[pl.ds(1, LON), pl.ds(STARTS[c], rows), :],
            in_sem.at[c],
        )
        copy.start()
        loads.append(copy)

    flags = mask_ref[...].astype(jnp.float32)
    for r in range(LON):
        wide = jnp.broadcast_to(flags[r:r + 1, :], (8, LAT))
        sea[r + 1] = wide
        live_ref[(r - 1) % LON] = wide
    order[pl.ds(0, LON - 1), :] = flags[1:, :]
    order[pl.ds(LON - 1, 1), :] = flags[:1, :]
    order[pl.ds(LON, 3), :] = jnp.zeros((3, LAT), jnp.float32)

    pl.semaphore_wait(barrier, 5)
    edges = []
    for slot, row, into, to in ((0, LON - 1, 0, east), (1, 0, LON + 1, west)):
        copy = pltpu.make_async_remote_copy(
            src_ref=spec_ref.at[row], dst_ref=x.at[into, pl.ds(0, LOCAL), :],
            send_sem=halo_send.at[slot], recv_sem=halo_recv.at[slot], device_id=(to, me), device_id_type=MESH,
        )
        copy.start()
        edges.append(copy)
        copy = pltpu.make_async_remote_copy(
            src_ref=sea.at[row + 1], dst_ref=sea.at[into],
            send_sem=halo_send.at[2 + slot], recv_sem=halo_recv.at[2 + slot], device_id=(to, me), device_id_type=MESH,
        )
        copy.start()
        edges.append(copy)

    dot = functools.partial(jnp.dot, preferred_element_type=jnp.float32)
    steps = LON + 3
    here = order[...]
    down = lax.broadcasted_iota(jnp.int32, (LAT, LAT), 0)
    across = lax.broadcasted_iota(jnp.int32, (LAT, LAT), 1)
    rank = dot(here, (down <= across).astype(jnp.float32))
    number = dot(here, jnp.ones((LAT, LAT), jnp.float32))
    before = lax.broadcasted_iota(jnp.int32, (steps, steps), 0) > lax.broadcasted_iota(jnp.int32, (steps, steps), 1)
    offset = dot(before.astype(jnp.float32), number).astype(jnp.int32)
    lane = lax.broadcasted_iota(jnp.int32, (steps, LAT), 1)
    step_of = lax.broadcasted_iota(jnp.int32, (steps, LAT), 0)
    reached = jnp.where((offset <= lane * LAT + (LAT - 1)) & (step_of <= LON), 1, 0)
    last_rows[...] = jnp.broadcast_to(jnp.sum(reached, axis=0, keepdims=True) - 1, (8, LAT))
    copy_last = pltpu.make_async_copy(last_rows, last, last_sem)
    copy_last.start()
    first_ref[...] = jnp.minimum(offset // LAT, TILES - 1)
    shift = offset % LAT
    for t in range(steps // 8):
        some = slice(8 * t, 8 * t + 8)
        ranks, moved_by = rank[some], shift[some]
        lanes = lane[some]
        wanted = ((lanes - moved_by + LAT) % LAT).astype(jnp.float32)
        position = jnp.zeros((8, LAT), jnp.int32)
        for half in (64, 32, 16, 8, 4, 2, 1):
            probe = jnp.take_along_axis(ranks, position + (half - 1), axis=1)
            position = jnp.where(probe <= wanted, position + half, position)
        low = (lanes >= moved_by).astype(jnp.int32)
        over = (moved_by.astype(jnp.float32) + number[some] >= LAT).astype(jnp.int32)
        place = (moved_by + ranks.astype(jnp.int32) + (LAT - 1)) % LAT
        for u in range(8):
            i = 8 * t + u
            if i < LON:
                for ref, value in ((source, position), (low_ref, low), (cross, over), (place_ref, place)):
                    ref[i] = jnp.broadcast_to(value[u:u + 1, :], (8, LAT))
                gust_ref[i] = jnp.broadcast_to(wind_ref[(i + 1) % LON:(i + 1) % LON + 1, :], (8, LAT))

    def own(ref):
        part = [ref[:, LOCAL * p:LOCAL * (p + 1)] for p in range(GROUPS)]
        return jnp.where(me < 2, jnp.where(me == 0, part[0], part[1]), jnp.where(me == 2, part[2], part[3]))

    def columns_of(row):
        row = jnp.concatenate([row, jnp.zeros((1, 3 * LAT - LOCAL), jnp.float32)], axis=1)
        return [jnp.broadcast_to(row[:, LAT * b:LAT * (b + 1)], (LAT, LAT)).T for b in range(3)]

    at_lat, at_weight, at_growth = columns_of(lat_ref[...]), columns_of(own(weight_ref)), columns_of(own(growth_ref))
    for b in range(3):
        rows = min(LAT, PADDED - LAT * b)
        real = min(LAT, LOCAL - LAT * b)
        to = pl.ds(LAT * b, rows)
        along = cour_ref[pl.ds(LAT * b, real), :]
        if real < rows:
            along = jnp.concatenate([along, jnp.zeros((rows - real, LAT), jnp.float32)], axis=0)
        up, down_by = jnp.maximum(along, 0.0), jnp.minimum(along, 0.0)
        lat = at_lat[b][:rows]
        north, south = jnp.maximum(lat, 0.0), jnp.minimum(lat, 0.0)
        lanes = lax.broadcasted_iota(jnp.int32, (rows, LAT), 1)
        coef[0, to, :] = 1.0 - up + down_by - north + south
        coef[1, to, :] = up
        coef[2, to, :] = -down_by
        coef[3, to, :] = jnp.where(lanes == 0, 0.0, north)
        coef[4, to, :] = jnp.where(lanes == LAT - 1, 0.0, -south)
        coef[5, to, :] = at_weight[b][:rows]
        grow_ref[to, :] = at_growth[b][:rows]

    steep[...] = jnp.zeros_like(steep)
    pad = PADDED - LOCAL
    x[:, pl.ds(LOCAL, pad), :] = jnp.zeros((LON + 2, pad, LAT), jnp.float32)

    def group_of(start, n, base, part):
        at = [pl.ds(pl.multiple_of(base + 8 * j, 8), 8) for j in range(n)]
        to = [pl.ds(pl.multiple_of(base - start + 8 * j, 8), 8) for j in range(n)]
        coefs = [[coef[q, at[j], :] for q in range(6)] for j in range(n)]

        def masked(row, j):
            return x[row, at[j], :] * sea[row]

        def treat(todo, sides, hold):
            stores = []
            for i, row, fresh in todo:
                land, turn, low, over, total = sea[row], source[i], low_ref[i] != 0, cross[i] != 0, steep[i]
                if fresh:
                    sides = [(masked(row - 1, j), masked(row, j)) for j in range(n)]
                new_hold = []
                for j in range(n):
                    c0, cw, ce, cs, cn, weight = coefs[j]
                    low_side, mid = sides[j]
                    high_side = masked(row + 1, j)
                    value = c0 * mid + cw * low_side + ce * high_side
                    value = value + cs * pltpu.roll(mid, 1, 1) + cn * pltpu.roll(mid, LAT - 1, 1)
                    value = value * land
                    total = total + weight * value
                    turned = jnp.take_along_axis(value, turn, axis=1)
                    kept = jnp.where(low, turned, hold[j])
                    stores.append((moved, row - 1, at[j], value))
                    stores.append((packed, i, to[j], kept))
                    new_hold.append(jnp.where(over, turned, kept))
                    sides[j] = (mid, high_side)
                stores.append((steep, i, slice(None), total))
                hold = new_hold
            for ref, i, rows, value in stores:
                ref[i, rows, :] = value
            return sides, hold

        if part != 1:
            sides = [(masked(1, j), masked(2, j)) for j in range(n)]
            hold = [jnp.zeros((8, LAT), jnp.float32) for j in range(n)]

            def several(s, carry):
                sides, hold = treat(
                    [(s * ROWS_AT_ONCE + u, s * ROWS_AT_ONCE + u + 2, False) for u in range(ROWS_AT_ONCE)],
                    list(carry[0]), list(carry[1]),
                )
                return (tuple(sides), tuple(hold))

            inner = LON - 2
            count = inner // ROWS_AT_ONCE
            sides, hold = lax.fori_loop(0, count, several, (tuple(sides), tuple(hold)))
            sides, hold = list(sides), list(hold)
            rest = [(i, i + 2, False) for i in range(count * ROWS_AT_ONCE, inner)]
        else:
            sides, rest = None, []
            hold = [packed[LON, to[j], :] for j in range(n)]
        if part != 0:
            rest = rest + [(LON - 2, LON, part == 1), (LON - 1, 1, True)]
        if rest:
            sides, hold = treat(rest, sides, hold)
        for j in range(n):
            packed[LON, to[j], :] = hold[j]

    sends = []
    stores = []
    for c in range(PARTS):
        start, size = STARTS[c], SIZES[c]
        n = 2 if size % 16 == 0 else 3
        loads[c].wait()
        for part in ((0, 1) if c == 0 else (None,)):
            if part == 1:
                for copy in edges:
                    copy.wait()

            def group(s, _, start=start, n=n, part=part):
                group_of(start, n, start + s * 8 * n, part)
                return 0

            lax.fori_loop(0, size // (8 * n), group, 0)
        rows = min(size, LOCAL - start)
        copy = pltpu.make_async_copy(
            moved.at[:, pl.ds(start, rows), :], moved_ref.at[:, pl.ds(start, rows), :], out_sem.at[c]
        )
        copy.start()
        stores.append(copy)
        if c == 0:
            copy_last.wait()
        recv = recv_b if c == PARTS - 1 else recv_a.at[c]
        mine = pl.ds(pl.multiple_of(me * size, 8), size)
        for d in (2, 1, 3, 0):
            to = peer(d)
            values = [
                packed[last[0, to * (SHARE // LAT) + k], pl.ds(0, size), :] for k in range(SHARE // LAT)
            ]
            for k in range(SHARE // LAT):
                lanes = pl.ds(k * LAT, LAT)
                if d == 0:
                    recv[mine, lanes] = values[k]
                else:
                    stage[d - 1, pl.ds(start, size), lanes] = values[k]
            if d:
                copy = pltpu.make_async_remote_copy(
                    src_ref=stage.at[d - 1, pl.ds(start, size), :], dst_ref=recv.at[mine, :],
                    send_sem=send_sem.at[c, d - 1], recv_sem=recv_sem.at[c, d - 1],
                    device_id=(block, to), device_id_type=MESH,
                )
                copy.start()
                sends.append((c, copy))

    sums[0] = jnp.sum(steep[...], axis=1)
    sum_copies = []
    for d in (1, 2, 3):
        copy = pltpu.make_async_remote_copy(
            src_ref=sums.at[0], dst_ref=sums.at[d], send_sem=sum_send.at[d - 1], recv_sem=sum_recv.at[d - 1],
            device_id=(block, peer(d)), device_id_type=MESH,
        )
        copy.start()
        sum_copies.append(copy)

    exact = functools.partial(jnp.dot, precision=lax.Precision.HIGHEST, preferred_element_type=jnp.float32)
    fcols[...] = exact(fmix_ref[...], fcol_ref[...])
    spread = exact(dmix_ref[...], dcol_ref[...])
    for j in range(4):
        dcols[pl.ds(j * ND, ND), :] = spread

    def matrix_rows(p, _):
        for g, (size, count) in enumerate(((144, 4), (144, 4), (48, 1))):
            for c in range(PARTS):
                width = GROUPS * SIZES[c]
                cols = pl.ds(KSTARTS[c], width)
                index = lax.broadcasted_iota(jnp.int32, (size, width), 0)
                rows = [fcols[pl.ds(p * 9 + 4 * g + j, 1), cols] for j in range(count)]
                if count == 1:
                    factor = jnp.where(index < ND, rows[0], 0.0)
                else:
                    factor = jnp.where(
                        index < 2 * ND,
                        jnp.where(index < ND, rows[0], rows[1]),
                        jnp.where(index < 3 * ND, rows[2], rows[3]),
                    )
                value = factor * dcols[pl.ds(0, size), cols]
                high = value.astype(jnp.bfloat16)
                low = (value - high.astype(jnp.float32)).astype(jnp.bfloat16)
                at = pl.ds(144 * g, size)
                if c == PARTS - 1:
                    w_hi_b[p, at, :] = high
                    w_lo_b[p, at, :] = low
                else:
                    w_hi_a[c, p, at, :] = high
                    w_lo_a[c, p, at, :] = low
        return 0

    lax.fori_loop(0, GROUPS, matrix_rows, 0)

    def halves(value):
        high = value.astype(jnp.bfloat16)
        return high, (value - high.astype(jnp.float32)).astype(jnp.bfloat16)

    for c in range(PARTS - 1):
        for at, copy in sends:
            if at == c:
                copy.wait_recv()

        def columns(s, _, c=c):
            lanes = pl.ds(pl.multiple_of(s * 256, 256), 256)
            high, low = halves(recv_a[c, :, lanes])

            def rows(p, _):
                value = dot(w_hi_a[c, p], high) + dot(w_lo_a[c, p], high) + dot(w_hi_a[c, p], low)
                if c:
                    value = value + acc[p, :, lanes]
                acc[p, :, lanes] = value
                return 0

            return lax.fori_loop(0, GROUPS, rows, 0)

        lax.fori_loop(0, SHARE // 256, columns, 0)

    for at, copy in sends:
        if at == PARTS - 1:
            copy.wait_recv()
    backs = []
    own_copy = None
    lanes_here = pl.ds(pl.multiple_of(me * SHARE, SHARE), SHARE)
    for d in (2, 1, 3, 0):
        p = peer(d)

        def columns(s, _, p=p):
            lanes = pl.ds(pl.multiple_of(s * 256, 256), 256)
            high, low = halves(recv_b[:, lanes])
            value = dot(w_hi_b[p], high) + dot(w_lo_b[p], high) + dot(w_hi_b[p], low)
            acc[p, :, lanes] = value + acc[p, :, lanes]
            return 0

        lax.fori_loop(0, SHARE // 256, columns, 0)
        if d:
            copy = pltpu.make_async_remote_copy(
                src_ref=acc.at[p, pl.ds(0, PADDED), :], dst_ref=mixed_ref.at[:, lanes_here],
                send_sem=back_send.at[d - 1], recv_sem=back_recv.at[d - 1],
                device_id=(block, p), device_id_type=MESH,
            )
            copy.start()
            backs.append(copy)
        else:
            own_copy = pltpu.make_async_copy(acc.at[p, pl.ds(0, PADDED), :], mixed_ref.at[:, lanes_here], own_sem)
            own_copy.start()

    for copy in sum_copies:
        copy.wait()
    whole = (sums[0] + sums[1]) + (sums[2] + sums[3])
    whole = 0.5 * whole / (1.0 + whole)
    for i in range(LON):
        damp_ref[i] = jnp.broadcast_to(whole[i:i + 1, :], (8, LAT))
    for copy in stores:
        copy.wait()
    for _, copy in sends:
        copy.wait_send()
    own_copy.wait()
    for copy in backs:
        copy.wait()


def finish_kernel(first_ref, moved_ref, mixed_ref, grow_ref, gust_ref, damp_ref, live_ref, low_ref, place_ref, out_ref):
    tiles = moved_ref.shape[1] // 8

    def treat(todo):
        stores = []
        for i, row in todo:
            first = first_ref[i, 0]
            here = pl.ds(pl.multiple_of(first * LAT, LAT), LAT)
            there = pl.ds(pl.multiple_of(jnp.minimum(first + 1, TILES - 1) * LAT, LAT), LAT)
            low, place, gust, damp, live = low_ref[i] != 0, place_ref[i], gust_ref[i], damp_ref[i], live_ref[i] != 0.0
            for j in range(tiles):
                at = pl.ds(8 * j, 8)
                joined = jnp.where(low, mixed_ref[at, here], mixed_ref[at, there])
                term = jnp.take_along_axis(joined, place, axis=1)
                value = moved_ref[row, at, :]
                source = value * (grow_ref[at, :] * gust - damp) + term
                stores.append((row, at, value + jnp.where(live, 0.5 * source, 0.0)))
        for row, at, value in stores:
            out_ref[row, at, :] = value

    def several(s, _):
        treat([(s * 4 + u, s * 4 + u + 1) for u in range(4)])
        return 0

    lax.fori_loop(0, (LON - 1) // 4, several, 0)
    treat([(LON - 1, 0)])


def on_device(
    spectrum, sea_mask, cour_lon, cour_lat, wind, growth_rate, band_weight, freq_mix, dir_mix, routes, counts
):
    spec = jnp.transpose(spectrum, (1, 0, 2))
    fcol, dcol = column_maps()
    f32, bf16, i32 = jnp.float32, jnp.bfloat16, jnp.int32
    vmem = pl.BlockSpec(memory_space=pltpu.VMEM)
    hbm = pl.BlockSpec(memory_space=pl.ANY)
    smem = pl.BlockSpec(memory_space=pltpu.SMEM)
    dma = pltpu.SemaphoreType.DMA
    wide = (LON, 8, LAT)
    moved, mixed, damp, gust, live, low, place, first, grow = pl.pallas_call(
        exchange_kernel,
        out_shape=(
            jax.ShapeDtypeStruct((LON, LOCAL, LAT), f32),
            jax.ShapeDtypeStruct((PADDED, CELLS), f32),
            jax.ShapeDtypeStruct(wide, f32),
            jax.ShapeDtypeStruct(wide, f32),
            jax.ShapeDtypeStruct(wide, f32),
            jax.ShapeDtypeStruct(wide, i32),
            jax.ShapeDtypeStruct(wide, i32),
            jax.ShapeDtypeStruct((LON + 3, LAT), i32),
            jax.ShapeDtypeStruct((PADDED, LAT), f32),
        ),
        in_specs=[hbm] + [vmem] * 10,
        out_specs=(hbm, hbm) + (vmem,) * 7,
        scratch_shapes=[
            pltpu.VMEM((LON + 2, PADDED, LAT), f32),
            pltpu.VMEM((LON, PADDED, LAT), f32),
            pltpu.VMEM((LON + 2, 8, LAT), f32),
            pltpu.VMEM(wide, i32),
            pltpu.VMEM(wide, i32),
            pltpu.VMEM((LON + 3, LAT), f32),
            pltpu.VMEM((8, LAT), i32),
            pltpu.SMEM((8, LAT), i32),
            pltpu.VMEM((6, PADDED, LAT), f32),
            pltpu.VMEM((LON + 1, max(SIZES), LAT), f32),
            pltpu.VMEM((GROUPS - 1, PADDED, SHARE), f32),
            pltpu.VMEM((PARTS - 1, GROUPS * SIZES[0], SHARE), f32),
            pltpu.VMEM((GROUPS * SIZES[-1], SHARE), f32),
            pltpu.VMEM((GROUPS, MROWS, SHARE), f32),
            pltpu.VMEM((PARTS - 1, GROUPS, MROWS, GROUPS * SIZES[0]), bf16),
            pltpu.VMEM((PARTS - 1, GROUPS, MROWS, GROUPS * SIZES[0]), bf16),
            pltpu.VMEM((GROUPS, MROWS, GROUPS * SIZES[-1]), bf16),
            pltpu.VMEM((GROUPS, MROWS, GROUPS * SIZES[-1]), bf16),
            pltpu.VMEM((NF, KTOTAL), f32),
            pltpu.VMEM((4 * ND, KTOTAL), f32),
            pltpu.VMEM(wide, f32),
            pltpu.VMEM((GROUPS, LON, LAT), f32),
            dma((PARTS,)), dma((PARTS,)), dma((4,)), dma((4,)), dma((PARTS, 3)), dma((PARTS, 3)),
            dma((3,)), dma((3,)), dma((3,)), dma((3,)), dma, dma,
        ],
        compiler_params=pltpu.CompilerParams(
            collective_id=0, has_side_effects=True, vmem_limit_bytes=56 << 20
        ),
    )(
        spec, sea_mask, cour_lon, cour_lat.reshape(1, LOCAL), wind,
        growth_rate.reshape(1, -1), band_weight.reshape(1, -1), freq_mix, dir_mix, jnp.asarray(fcol), jnp.asarray(dcol),
    )
    step = 88
    whole = pl.BlockSpec(wide, lambda c: (0, 0, 0))
    out = pl.pallas_call(
        finish_kernel,
        out_shape=jax.ShapeDtypeStruct((LON, LOCAL, LAT), f32),
        grid=(pl.cdiv(LOCAL, step),),
        in_specs=[
            smem,
            pl.BlockSpec((LON, step, LAT), lambda c: (0, c, 0)),
            pl.BlockSpec((step, CELLS), lambda c: (c, 0)),
            pl.BlockSpec((step, LAT), lambda c: (c, 0)),
            whole, whole, whole, whole, whole,
        ],
        out_specs=pl.BlockSpec((LON, step, LAT), lambda c: (0, c, 0)),
        compiler_params=pltpu.CompilerParams(vmem_limit_bytes=58 << 20),
    )(first, moved, mixed, grow, gust, damp, live, low, place)
    return jnp.transpose(out, (1, 0, 2))


def solution(mesh):
    placed = (
        P("bin", "lon", None),
        P("lon", None),
        P("bin", None),
        P("bin"),
        P("lon", None),
        P(),
        P(),
        P(),
        P(),
        P("lon", None, None),
        P("lon", None),
    )
    return jax.shard_map(
        on_device, mesh=mesh, in_specs=placed, out_specs=P("bin", "lon", None), check_vma=False
    )
```

```python
import functools

import jax
import jax.numpy as jnp
import numpy as np
from jax import lax
from jax.experimental import pallas as pl
from jax.experimental.pallas import tpu as pltpu
from jax.sharding import PartitionSpec as P

MESH = pl.DeviceIdType.MESH
dissipation = 0.5
time_step = 0.5
NF, ND = 36, 36
LON, LAT = 45, 128
GROUPS = 4
LOCAL = 324
PADDED = 328
CELLS = 4096
SHARE = CELLS // GROUPS
TILES = CELLS // LAT
SIZES = (64, 64, 64, 64, 72)
STARTS = (0, 64, 128, 192, 256)
PARTS = len(SIZES)
KSTARTS = tuple(GROUPS * s for s in STARTS)
KTOTAL = GROUPS * PADDED
MROWS = 336
OWN = SHARE // LAT
HALF = OWN // 2
ROWS_AT_ONCE = 10


def column_maps():
    freq = np.zeros((NF, KTOTAL), np.float32)
    direction = np.zeros((ND, KTOTAL), np.float32)
    at = 0
    for start, size in zip(STARTS, SIZES):
        for p in range(GROUPS):
            for b in range(start, start + size):
                if b < LOCAL:
                    k = p * LOCAL + b
                    freq[k // ND, at] = 1.0
                    direction[k % ND, at] = 1.0
                at += 1
    return freq, direction


def exchange_kernel(
    spec_ref, mask_ref, cour_ref, wind_ref, bins_ref, fmix_ref, dmix_ref, fcol_ref, dcol_ref,
    moved_ref, mixed_ref, live_ref, low_ref, place_ref, first_ref,
    x, moved, sea, gust, damp, source, cross, head, order, last_rows, last, coef, grow, packed, edge, stage, recv, tail, acc,
    w_hi, w_lo, f_hi, f_lo, fcols, dcols, steep, sums,
    in_sem, halo_send, halo_recv, send_sem, recv_sem, back_send, back_recv, sum_send, sum_recv, own_sem, last_sem, out_sem,
):
    me = lax.axis_index("bin")
    block = lax.axis_index("lon")
    blocks = lax.axis_size("lon")
    west = lax.rem(block + blocks - 1, blocks)
    east = lax.rem(block + 1, blocks)

    def peer(d):
        return lax.rem(me + d, GROUPS)

    barrier = pltpu.get_barrier_semaphore()
    for d in (1, 2, 3):
        pl.semaphore_signal(barrier, inc=1, device_id=(block, peer(d)), device_id_type=MESH)
    pl.semaphore_signal(barrier, inc=1, device_id=(west, me), device_id_type=MESH)
    pl.semaphore_signal(barrier, inc=1, device_id=(east, me), device_id_type=MESH)

    loads = []
    for c in range(PARTS):
        rows = min(SIZES[c], LOCAL - STARTS[c])
        copy = pltpu.make_async_copy(
            spec_ref.at[:, pl.ds(STARTS[c], rows), :],
            x.at[pl.ds(1, LON), pl.ds(STARTS[c], rows), :],
            in_sem.at[c],
        )
        copy.start()
        loads.append(copy)

    flags = mask_ref[...].astype(jnp.float32)
    for r in range(LON):
        wide = jnp.broadcast_to(flags[r:r + 1, :], (8, LAT))
        sea[r + 1] = wide
        live_ref[(r + 1) % LON] = wide
    order[pl.ds(0, 1), :] = flags[LON - 1:, :]
    order[pl.ds(1, LON - 1), :] = flags[:LON - 1, :]
    order[pl.ds(LON, 3), :] = jnp.zeros((3, LAT), jnp.float32)

    dot = functools.partial(jnp.dot, preferred_element_type=jnp.float32)
    steps = LON + 3
    here = order[...]
    down = lax.broadcasted_iota(jnp.int32, (LAT, LAT), 0)
    across = lax.broadcasted_iota(jnp.int32, (LAT, LAT), 1)
    rank = dot(here, (down <= across).astype(jnp.float32))
    number = dot(here, jnp.ones((LAT, LAT), jnp.float32))
    before = lax.broadcasted_iota(jnp.int32, (steps, steps), 0) > lax.broadcasted_iota(jnp.int32, (steps, steps), 1)
    offset = dot(before.astype(jnp.float32), number).astype(jnp.int32)
    lane = lax.broadcasted_iota(jnp.int32, (steps, LAT), 1)
    step_of = lax.broadcasted_iota(jnp.int32, (steps, LAT), 0)
    reached = jnp.where((offset <= lane * LAT + (LAT - 1)) & (step_of <= LON), 1, 0)
    last_rows[...] = jnp.broadcast_to(jnp.sum(reached, axis=0, keepdims=True) - 1, (8, LAT))
    copy_last = pltpu.make_async_copy(last_rows, last, last_sem)
    copy_last.start()
    first_ref[...] = jnp.minimum(offset // LAT, TILES - 1)
    shift = offset % LAT
    for t in range(steps // 8):
        some = slice(8 * t, 8 * t + 8)
        ranks, moved_by = rank[some], shift[some]
        lanes = lane[some]
        wanted = ((lanes - moved_by + LAT) % LAT).astype(jnp.float32)
        position = jnp.zeros((8, LAT), jnp.int32)
        for half in (64, 32, 16, 8, 4, 2, 1):
            probe = jnp.take_along_axis(ranks, position + (half - 1), axis=1)
            position = jnp.where(probe <= wanted, position + half, position)
        low = (lanes >= moved_by).astype(jnp.int32)
        over = (moved_by.astype(jnp.float32) + number[some] >= LAT).astype(jnp.int32)
        place = (moved_by + ranks.astype(jnp.int32) + (LAT - 1)) % LAT
        for u in range(8):
            i = 8 * t + u
            if i < LON:
                for ref, value in ((source, position), (low_ref, low), (cross, over), (place_ref, place)):
                    ref[i] = jnp.broadcast_to(value[u:u + 1, :], (8, LAT))
                r = (i - 1) % LON
                gust[i] = jnp.broadcast_to(wind_ref[r:r + 1, :], (8, LAT))

    lanes = lane[:8]
    first_cells, edge_cells = offset[1:2, :], offset[2:3, :]
    head[0] = (lanes < first_cells).astype(jnp.int32)
    head[1] = (lanes < edge_cells).astype(jnp.int32)
    head[2] = (lanes + LAT < edge_cells).astype(jnp.int32)

    def own(at):
        part = [bins_ref[:, at + LOCAL * p:at + LOCAL * (p + 1)] for p in range(GROUPS)]
        return jnp.where(me < 2, jnp.where(me == 0, part[0], part[1]), jnp.where(me == 2, part[2], part[3]))

    def columns_of(row):
        row = jnp.concatenate([row, jnp.zeros((1, 3 * LAT - LOCAL), jnp.float32)], axis=1)
        return [jnp.broadcast_to(row[:, LAT * b:LAT * (b + 1)], (LAT, LAT)).T for b in range(3)]

    at_lat, at_weight, at_growth = columns_of(bins_ref[:, :LOCAL]), columns_of(own(LOCAL)), columns_of(own(5 * LOCAL))
    for b in range(3):
        rows = min(LAT, PADDED - LAT * b)
        real = min(LAT, LOCAL - LAT * b)
        to = pl.ds(LAT * b, rows)
        along = cour_ref[pl.ds(LAT * b, real), :]
        if real < rows:
            along = jnp.concatenate([along, jnp.zeros((rows - real, LAT), jnp.float32)], axis=0)
        up, down_by = jnp.maximum(along, 0.0), jnp.minimum(along, 0.0)
        lat = at_lat[b][:rows]
        north, south = jnp.maximum(lat, 0.0), jnp.minimum(lat, 0.0)
        lanes = lax.broadcasted_iota(jnp.int32, (rows, LAT), 1)
        coef[0, to, :] = 1.0 - up + down_by - north + south
        coef[1, to, :] = up
        coef[2, to, :] = -down_by
        coef[3, to, :] = jnp.where(lanes == 0, 0.0, north)
        coef[4, to, :] = jnp.where(lanes == LAT - 1, 0.0, -south)
        coef[5, to, :] = at_weight[b][:rows]
        grow[to, :] = at_growth[b][:rows]

    steep[...] = jnp.zeros_like(steep)
    pad = PADDED - LOCAL
    x[:, pl.ds(LOCAL, pad), :] = jnp.zeros((LON + 2, pad, LAT), jnp.float32)
    for p in range(GROUPS):
        tail[p, :, pl.ds(SIZES[-1] - pad, pad), :] = jnp.zeros((OWN, pad, LAT), jnp.float32)
    packed[pl.ds(0, 2)] = jnp.zeros((2,) + packed.shape[1:], jnp.float32)

    def tiles_of(start, n, base):
        at = [pl.ds(pl.multiple_of(base + 8 * j, 8), 8) for j in range(n)]
        to = [pl.ds(pl.multiple_of(base - start + 8 * j, 8), 8) for j in range(n)]
        return at, to, [[coef[q, at[j], :] for q in range(6)] for j in range(n)]

    def masked(row, rows):
        return x[row, rows, :] * sea[row]

    def upwind(coefs, low_side, mid, high_side, land):
        c0, cw, ce, cs, cn, _ = coefs
        value = c0 * mid + cw * low_side + ce * high_side
        value = value + cs * pltpu.roll(mid, 1, 1) + cn * pltpu.roll(mid, LAT - 1, 1)
        return value * land

    def inner(start, n, base):
        at, to, coefs = tiles_of(start, n, base)

        def treat(steps, sides, hold):
            stores = []
            for i in steps:
                land, turn, low, over, total = sea[i], source[i], low_ref[i] != 0, cross[i] != 0, steep[i]
                new_hold = []
                for j in range(n):
                    low_side, mid = sides[j]
                    high_side = masked(i + 1, at[j])
                    value = upwind(coefs[j], low_side, mid, high_side, land)
                    total = total + coefs[j][5] * value
                    turned = jnp.take_along_axis(value, turn, axis=1)
                    kept = jnp.where(low, turned, hold[j])
                    stores.append((moved, i - 1, at[j], value))
                    stores.append((packed, i, to[j], kept))
                    new_hold.append(jnp.where(over, turned, kept))
                    sides[j] = (mid, high_side)
                stores.append((steep, i, slice(None), total))
                hold = new_hold
            for ref, i, rows, value in stores:
                ref[i, rows, :] = value
            return sides, hold

        def several(s, carry):
            sides, hold = treat(
                [2 + s * ROWS_AT_ONCE + u for u in range(ROWS_AT_ONCE)], list(carry[0]), list(carry[1])
            )
            return (tuple(sides), tuple(hold))

        sides = tuple((masked(1, at[j]), masked(2, at[j])) for j in range(n))
        hold = tuple(jnp.zeros((8, LAT), jnp.float32) for j in range(n))
        count = (LON - 2) // ROWS_AT_ONCE
        sides, hold = lax.fori_loop(0, count, several, (sides, hold))
        _, hold = treat(list(range(2 + count * ROWS_AT_ONCE, LON)), list(sides), list(hold))
        for j in range(n):
            packed[LON, to[j], :] = hold[j]

    def outer(start, n, base):
        at, to, coefs = tiles_of(start, n, base)
        first_cells = head[0] != 0
        totals = [steep[0], steep[1]]
        stores = []
        for j in range(n):
            turned = []
            for i, row in ((0, LON), (1, 1)):
                value = upwind(coefs[j], masked(row - 1, at[j]), masked(row, at[j]), masked(row + 1, at[j]), sea[row])
                totals[i] = totals[i] + coefs[j][5] * value
                stores.append((moved, row - 1, at[j], value))
                turned.append(jnp.take_along_axis(value, source[i], axis=1))
            stores.append((edge, 0, to[j], jnp.where(first_cells, turned[0], turned[1])))
            stores.append((edge, 1, to[j], turned[1]))
        for ref, i, rows, value in stores:
            ref[i, rows, :] = value
        steep[0], steep[1] = totals

    def landing(c):
        if c == PARTS - 1:
            return tail.at[me]
        return recv.at[:, pl.ds(pl.multiple_of(KSTARTS[c] + me * SIZES[c], 8), SIZES[c]), :]

    sends = {}

    def send(c, half):
        start, size = STARTS[c], SIZES[c]
        rows = min(size, LOCAL - start)
        tiles = pl.ds(HALF * (1 - half), HALF)
        for d in (2, 1, 3):
            copy = pltpu.make_async_remote_copy(
                src_ref=stage.at[d - 1, tiles, pl.ds(start, rows), :],
                dst_ref=landing(c).at[tiles, pl.ds(0, rows), :],
                send_sem=send_sem.at[half, c, d - 1], recv_sem=recv_sem.at[half, c, d - 1],
                device_id=(block, peer(d)), device_id_type=MESH,
            )
            copy.start()
            sends[half, c, d] = copy

    edges = []
    for c in range(PARTS):
        start, size = STARTS[c], SIZES[c]
        n = 2 if size % 16 == 0 else 3
        loads[c].wait()

        def group(s, _, start=start, n=n):
            inner(start, n, start + s * 8 * n)
            return 0

        lax.fori_loop(0, size // (8 * n), group, 0)
        if c == 0:
            copy_last.wait()
        mine = landing(c)
        for d in (2, 1, 3, 0):
            to = peer(d)
            values = [
                packed[last[0, to * OWN + k], pl.ds(0, size), :] for k in range(OWN)
            ]
            for k in range(OWN):
                if d == 0:
                    mine[k] = values[k]
                else:
                    stage[d - 1, k, pl.ds(start, size), :] = values[k]
        if c == 0:
            pl.semaphore_wait(barrier, 5)
            for slot, row, into, to in ((0, LON - 1, 0, east), (1, 0, LON + 1, west)):
                for k, src, dst in (
                    (slot, spec_ref.at[row], x.at[into, pl.ds(0, LOCAL), :]),
                    (2 + slot, sea.at[row + 1], sea.at[into]),
                ):
                    copy = pltpu.make_async_remote_copy(
                        src_ref=src, dst_ref=dst, send_sem=halo_send.at[k], recv_sem=halo_recv.at[k],
                        device_id=(to, me), device_id_type=MESH,
                    )
                    copy.start()
                    edges.append(copy)
        send(c, 0)

    for copy in edges:
        copy.wait()
    for c in range(PARTS):
        start, size = STARTS[c], SIZES[c]
        n = 2 if size % 16 == 0 else 3

        def group(s, _, start=start, n=n):
            outer(start, n, start + s * 8 * n)
            return 0

        lax.fori_loop(0, size // (8 * n), group, 0)
        for d in (2, 1, 3, 0):
            here = jnp.where(peer(d) == 0, 1, 0)
            share = landing(c) if d == 0 else stage.at[d - 1, :, pl.ds(start, size), :]
            for k in range(2):
                old = share[k]
                use = jnp.broadcast_to((head[1 + k] * here)[:1, :], (size, LAT)) != 0
                new = jnp.where(use, edge[k, pl.ds(0, size), :], old)
                share[k] = new
        send(c, 1)

    sums[0] = jnp.sum(steep[...], axis=1)
    sum_copies = []
    for d in (1, 2, 3):
        copy = pltpu.make_async_remote_copy(
            src_ref=sums.at[0], dst_ref=sums.at[d], send_sem=sum_send.at[d - 1], recv_sem=sum_recv.at[d - 1],
            device_id=(block, peer(d)), device_id_type=MESH,
        )
        copy.start()
        sum_copies.append(copy)

    exact = functools.partial(jnp.dot, precision=lax.Precision.HIGHEST, preferred_element_type=jnp.float32)
    fcols[...] = exact(fmix_ref[...], fcol_ref[...])
    spread = time_step * exact(dmix_ref[...], dcol_ref[...])
    for j in range(4):
        dcols[pl.ds(j * ND, ND), :] = spread

    def matrix_rows(p, _):
        for g, (size, count) in enumerate(((144, 4), (144, 4), (48, 1))):
            for c in range(PARTS):
                width = GROUPS * SIZES[c]
                cols = pl.ds(KSTARTS[c], width)
                index = lax.broadcasted_iota(jnp.int32, (size, width), 0)
                rows = [fcols[pl.ds(p * 9 + 4 * g + j, 1), cols] for j in range(count)]
                if count == 1:
                    factor = jnp.where(index < ND, rows[0], 0.0)
                else:
                    factor = jnp.where(
                        index < 2 * ND,
                        jnp.where(index < ND, rows[0], rows[1]),
                        jnp.where(index < 3 * ND, rows[2], rows[3]),
                    )
                value = factor * dcols[pl.ds(0, size), cols]
                high = value.astype(jnp.bfloat16)
                low = (value - high.astype(jnp.float32)).astype(jnp.bfloat16)
                at = pl.ds(144 * g, size)
                w_hi[p, at, cols] = high
                w_lo[p, at, cols] = low
        return 0

    lax.fori_loop(0, GROUPS, matrix_rows, 0)

    def arrive(half):
        for c in range(PARTS):
            for d in (1, 2, 3):
                sends[half, c, d].wait_recv()

    def mix(half):
        for s in range(HALF // 2):
            k = HALF * (1 - half) + 2 * s
            for c in range(PARTS):
                rows = pl.ds(KSTARTS[c], GROUPS * SIZES[c])
                if c == PARTS - 1:
                    both = [jnp.concatenate([tail[p, k + u] for p in range(GROUPS)], axis=0) for u in range(2)]
                else:
                    both = [recv[k + u, rows, :] for u in range(2)]
                value = jnp.concatenate(both, axis=1)
                high = value.astype(jnp.bfloat16)
                f_hi[rows, :] = high
                f_lo[rows, :] = (value - high.astype(jnp.float32)).astype(jnp.bfloat16)

            def rows_of(p, _, k=k):
                value = dot(w_hi[p], f_hi[...]) + dot(w_lo[p], f_hi[...]) + dot(w_hi[p], f_lo[...])
                acc[p, k] = value[:, :LAT]
                acc[p, k + 1] = value[:, LAT:]
                return 0

            lax.fori_loop(0, GROUPS, rows_of, 0)

    backs = []

    def send_back(half, d):
        p = peer(d)
        src = acc.at[p, pl.ds(HALF * (1 - half), HALF), pl.ds(0, LOCAL), :]
        tiles = pl.ds(me * OWN + HALF * (1 - half), HALF)
        if d == 0:
            copy = pltpu.make_async_copy(src, mixed_ref.at[tiles], own_sem.at[half])
        else:
            copy = pltpu.make_async_remote_copy(
                src_ref=src, dst_ref=mixed_ref.at[tiles],
                send_sem=back_send.at[half, d - 1], recv_sem=back_recv.at[half, d - 1],
                device_id=(block, p), device_id_type=MESH,
            )
        copy.start()
        backs.append(copy)

    arrive(0)
    mix(0)
    send_back(0, 2)
    arrive(1)
    for d in (1, 3, 0):
        send_back(0, d)
    mix(1)
    for d in (2, 1, 3, 0):
        send_back(1, d)

    for copy in sum_copies:
        copy.wait()
    whole = (sums[0] + sums[1]) + (sums[2] + sums[3])
    whole = dissipation * whole / (1.0 + whole)
    for i in range(LON):
        damp[i] = jnp.broadcast_to(whole[i:i + 1, :], (8, LAT))

    def add_own(i, row):
        keep = time_step * live_ref[i]
        gusts, damps = gust[i], damp[i]
        values = []
        for t in range(PADDED // 8):
            value = moved[row, pl.ds(8 * t, 8), :]
            values.append(value + keep * (value * (grow[pl.ds(8 * t, 8), :] * gusts - damps)))
        for t in range(PADDED // 8):
            moved[row, pl.ds(8 * t, 8), :] = values[t]

    def rows_own(i, _):
        add_own(i, i - 1)
        return 0

    lax.fori_loop(1, LON, rows_own, 0)
    add_own(0, LON - 1)
    store = pltpu.make_async_copy(moved.at[:, pl.ds(0, LOCAL), :], moved_ref, out_sem)
    store.start()
    store.wait()
    for copy in sends.values():
        copy.wait_send()
    for copy in backs:
        copy.wait()


def finish_kernel(first_ref, moved_ref, mixed_ref, live_ref, low_ref, place_ref, out_ref):
    tiles = moved_ref.shape[1] // 8

    def treat(todo):
        stores = []
        for i, row in todo:
            first = first_ref[i, 0]
            after = jnp.minimum(first + 1, TILES - 1)
            low, place, live = low_ref[i] != 0, place_ref[i], live_ref[i] != 0.0
            for j in range(tiles):
                at = pl.ds(8 * j, 8)
                joined = jnp.where(low, mixed_ref[first, at, :], mixed_ref[after, at, :])
                term = jnp.take_along_axis(joined, place, axis=1)
                stores.append((row, at, moved_ref[row, at, :] + jnp.where(live, term, 0.0)))
        for row, at, value in stores:
            out_ref[row, at, :] = value

    def several(s, _):
        treat([(s * 4 + u + 1, s * 4 + u) for u in range(4)])
        return 0

    lax.fori_loop(0, (LON - 1) // 4, several, 0)
    treat([(0, LON - 1)])


def on_device(
    spectrum, sea_mask, cour_lon, cour_lat, wind, growth_rate, band_weight, freq_mix, dir_mix, routes, counts
):
    spec = jnp.transpose(spectrum, (1, 0, 2))
    fcol, dcol = column_maps()
    f32, bf16, i32 = jnp.float32, jnp.bfloat16, jnp.int32
    vmem = pl.BlockSpec(memory_space=pltpu.VMEM)
    hbm = pl.BlockSpec(memory_space=pl.ANY)
    smem = pl.BlockSpec(memory_space=pltpu.SMEM)
    dma = pltpu.SemaphoreType.DMA
    wide = (LON, 8, LAT)
    moved, mixed, live, low, place, first = pl.pallas_call(
        exchange_kernel,
        out_shape=(
            jax.ShapeDtypeStruct((LON, LOCAL, LAT), f32),
            jax.ShapeDtypeStruct((TILES, LOCAL, LAT), f32),
            jax.ShapeDtypeStruct(wide, f32),
            jax.ShapeDtypeStruct(wide, i32),
            jax.ShapeDtypeStruct(wide, i32),
            jax.ShapeDtypeStruct((LON + 3, LAT), i32),
        ),
        in_specs=[hbm] + [vmem] * 8,
        out_specs=(hbm, hbm) + (vmem,) * 4,
        scratch_shapes=[
            pltpu.VMEM((LON + 2, PADDED, LAT), f32),
            pltpu.VMEM((LON, PADDED, LAT), f32),
            pltpu.VMEM((LON + 2, 8, LAT), f32),
            pltpu.VMEM(wide, f32),
            pltpu.VMEM(wide, f32),
            pltpu.VMEM(wide, i32),
            pltpu.VMEM(wide, i32),
            pltpu.VMEM((3, 8, LAT), i32),
            pltpu.VMEM((LON + 3, LAT), f32),
            pltpu.VMEM((8, LAT), i32),
            pltpu.SMEM((8, LAT), i32),
            pltpu.VMEM((6, PADDED, LAT), f32),
            pltpu.VMEM((PADDED, LAT), f32),
            pltpu.VMEM((LON + 1, max(SIZES), LAT), f32),
            pltpu.VMEM((2, max(SIZES), LAT), f32),
            pltpu.VMEM((GROUPS - 1, OWN, PADDED, LAT), f32),
            pltpu.VMEM((OWN, KSTARTS[-1], LAT), f32),
            pltpu.VMEM((GROUPS, OWN, SIZES[-1], LAT), f32),
            pltpu.VMEM((GROUPS, OWN, MROWS, LAT), f32),
            pltpu.VMEM((GROUPS, MROWS, KTOTAL), bf16),
            pltpu.VMEM((GROUPS, MROWS, KTOTAL), bf16),
            pltpu.VMEM((KTOTAL, 256), bf16),
            pltpu.VMEM((KTOTAL, 256), bf16),
            pltpu.VMEM((NF, KTOTAL), f32),
            pltpu.VMEM((4 * ND, KTOTAL), f32),
            pltpu.VMEM(wide, f32),
            pltpu.VMEM((GROUPS, LON, LAT), f32),
            dma((PARTS,)), dma((4,)), dma((4,)), dma((2, PARTS, 3)), dma((2, PARTS, 3)),
            dma((2, 3)), dma((2, 3)), dma((3,)), dma((3,)), dma((2,)), dma, dma,
        ],
        compiler_params=pltpu.CompilerParams(
            collective_id=0, has_side_effects=True, vmem_limit_bytes=56 << 20
        ),
    )(
        spec, sea_mask, cour_lon, wind,
        jnp.concatenate([cour_lat, band_weight, growth_rate]).reshape(1, -1), freq_mix, dir_mix, jnp.asarray(fcol), jnp.asarray(dcol),
    )
    step = 88
    whole = pl.BlockSpec(wide, lambda c: (0, 0, 0))
    out = pl.pallas_call(
        finish_kernel,
        out_shape=jax.ShapeDtypeStruct((LON, LOCAL, LAT), f32),
        grid=(pl.cdiv(LOCAL, step),),
        in_specs=[
            smem,
            pl.BlockSpec((LON, step, LAT), lambda c: (0, c, 0)),
            pl.BlockSpec((TILES, step, LAT), lambda c: (0, c, 0)),
            whole, whole, whole,
        ],
        out_specs=pl.BlockSpec((LON, step, LAT), lambda c: (0, c, 0)),
        compiler_params=pltpu.CompilerParams(vmem_limit_bytes=58 << 20),
    )(first, moved, mixed, live, low, place)
    return jnp.transpose(out, (1, 0, 2))


def solution(mesh):
    placed = (
        P("bin", "lon", None),
        P("lon", None),
        P("bin", None),
        P("bin"),
        P("lon", None),
        P(),
        P(),
        P(),
        P(),
        P("lon", None, None),
        P("lon", None),
    )
    return jax.shard_map(
        on_device, mesh=mesh, in_specs=placed, out_specs=P("bin", "lon", None), check_vma=False
    )
```

```python
import functools

import jax
import jax.numpy as jnp
import numpy as np
from jax import lax
from jax.experimental import pallas as pl
from jax.experimental.pallas import tpu as pltpu
from jax.sharding import PartitionSpec as P

MESH = pl.DeviceIdType.MESH
dissipation = 0.5
time_step = 0.5
NF, ND = 36, 36
LON, LAT = 45, 128
GROUPS = 4
LOCAL = 324
PADDED = 328
CELLS = 4096
SHARE = CELLS // GROUPS
TILES = CELLS // LAT
SIZES = (16, 32, 48, 96, 136)
STARTS = (0, 16, 48, 96, 192)
PARTS = len(SIZES)
KSTARTS = tuple(GROUPS * s for s in STARTS)
KTOTAL = GROUPS * PADDED
MROWS = 336
OWN = SHARE // LAT
HALF = OWN // 2
ROWS_AT_ONCE = 10


def column_maps():
    freq = np.zeros((NF, KTOTAL), np.float32)
    direction = np.zeros((ND, KTOTAL), np.float32)
    at = 0
    for start, size in zip(STARTS, SIZES):
        for p in range(GROUPS):
            for b in range(start, start + size):
                if b < LOCAL:
                    k = p * LOCAL + b
                    freq[k // ND, at] = 1.0
                    direction[k % ND, at] = 1.0
                at += 1
    return freq, direction


def exchange_kernel(
    spec_ref, mask_ref, cour_hbm, wind_ref, bins_ref, fmix_ref, dmix_ref, fcol_hbm, dcol_hbm,
    moved_ref, mixed_ref, live_out, low_out, place_out, first_out,
    cour_ref, fcol_ref, dcol_ref, live_ref, low_ref, place_ref, first_ref,
    x, moved, sea, gust, damp, source, cross, head, order, last_rows, last, coef, grow, packed, edge, stage, recv, tail, acc,
    w_hi, w_lo, f_hi, f_lo, fcols, dcols, steep, sums,
    in_sem, halo_send, halo_recv, send_sem, recv_sem, back_send, back_recv, sum_send, sum_recv, own_sem, last_sem, out_sem,
    early_sem, late_sem,
):
    me = lax.axis_index("bin")
    block = lax.axis_index("lon")
    blocks = lax.axis_size("lon")
    west = lax.rem(block + blocks - 1, blocks)
    east = lax.rem(block + 1, blocks)

    def peer(d):
        return lax.rem(me + d, GROUPS)

    barrier = pltpu.get_barrier_semaphore()
    for d in (1, 2, 3):
        pl.semaphore_signal(barrier, inc=1, device_id=(block, peer(d)), device_id_type=MESH)
    pl.semaphore_signal(barrier, inc=1, device_id=(west, me), device_id_type=MESH)
    pl.semaphore_signal(barrier, inc=1, device_id=(east, me), device_id_type=MESH)

    early = [
        pltpu.make_async_copy(src, dst, early_sem.at[q])
        for q, (src, dst) in enumerate(((cour_hbm, cour_ref), (fcol_hbm, fcol_ref), (dcol_hbm, dcol_ref)))
    ]
    early[0].start()

    loads = []
    for c in range(PARTS):
        rows = min(SIZES[c], LOCAL - STARTS[c])
        copy = pltpu.make_async_copy(
            spec_ref.at[:, pl.ds(STARTS[c], rows), :],
            x.at[pl.ds(1, LON), pl.ds(STARTS[c], rows), :],
            in_sem.at[c],
        )
        copy.start()
        loads.append(copy)

    for copy in early[1:]:
        copy.start()

    flags = mask_ref[...].astype(jnp.float32)
    for r in range(LON):
        wide = jnp.broadcast_to(flags[r:r + 1, :], (8, LAT))
        sea[r + 1] = wide
        live_ref[(r + 1) % LON] = wide
    order[pl.ds(0, 1), :] = flags[LON - 1:, :]
    order[pl.ds(1, LON - 1), :] = flags[:LON - 1, :]
    order[pl.ds(LON, 3), :] = jnp.zeros((3, LAT), jnp.float32)

    dot = functools.partial(jnp.dot, preferred_element_type=jnp.float32)
    steps = LON + 3
    here = order[...]
    down = lax.broadcasted_iota(jnp.int32, (LAT, LAT), 0)
    across = lax.broadcasted_iota(jnp.int32, (LAT, LAT), 1)
    rank = dot(here, (down <= across).astype(jnp.float32))
    number = dot(here, jnp.ones((LAT, LAT), jnp.float32))
    before = lax.broadcasted_iota(jnp.int32, (steps, steps), 0) > lax.broadcasted_iota(jnp.int32, (steps, steps), 1)
    offset = dot(before.astype(jnp.float32), number).astype(jnp.int32)
    lane = lax.broadcasted_iota(jnp.int32, (steps, LAT), 1)
    step_of = lax.broadcasted_iota(jnp.int32, (steps, LAT), 0)
    reached = jnp.where((offset <= lane * LAT + (LAT - 1)) & (step_of <= LON), 1, 0)
    last_rows[...] = jnp.broadcast_to(jnp.sum(reached, axis=0, keepdims=True) - 1, (8, LAT))
    copy_last = pltpu.make_async_copy(last_rows, last, last_sem)
    copy_last.start()
    first_ref[...] = jnp.minimum(offset // LAT, TILES - 1)
    shift = offset % LAT
    for t in range(steps // 8):
        some = slice(8 * t, 8 * t + 8)
        ranks, moved_by = rank[some], shift[some]
        lanes = lane[some]
        wanted = ((lanes - moved_by + LAT) % LAT).astype(jnp.float32)
        position = jnp.zeros((8, LAT), jnp.int32)
        for half in (64, 32, 16, 8, 4, 2, 1):
            probe = jnp.take_along_axis(ranks, position + (half - 1), axis=1)
            position = jnp.where(probe <= wanted, position + half, position)
        low = (lanes >= moved_by).astype(jnp.int32)
        over = (moved_by.astype(jnp.float32) + number[some] >= LAT).astype(jnp.int32)
        place = (moved_by + ranks.astype(jnp.int32) + (LAT - 1)) % LAT
        for u in range(8):
            i = 8 * t + u
            if i < LON:
                for ref, value in ((source, position), (low_ref, low), (cross, over), (place_ref, place)):
                    ref[i] = jnp.broadcast_to(value[u:u + 1, :], (8, LAT))
                r = (i - 1) % LON
                gust[i] = jnp.broadcast_to(wind_ref[r:r + 1, :], (8, LAT))

    late = [
        pltpu.make_async_copy(src, dst, late_sem.at[q])
        for q, (src, dst) in enumerate(
            ((live_ref, live_out), (low_ref, low_out), (place_ref, place_out), (first_ref, first_out))
        )
    ]
    for copy in late:
        copy.start()

    lanes = lane[:8]
    first_cells, edge_cells = offset[1:2, :], offset[2:3, :]
    head[0] = (lanes < first_cells).astype(jnp.int32)
    head[1] = (lanes < edge_cells).astype(jnp.int32)
    head[2] = (lanes + LAT < edge_cells).astype(jnp.int32)

    def own(at):
        part = [bins_ref[:, at + LOCAL * p:at + LOCAL * (p + 1)] for p in range(GROUPS)]
        return jnp.where(me < 2, jnp.where(me == 0, part[0], part[1]), jnp.where(me == 2, part[2], part[3]))

    def columns_of(row):
        row = jnp.concatenate([row, jnp.zeros((1, 3 * LAT - LOCAL), jnp.float32)], axis=1)
        return [jnp.broadcast_to(row[:, LAT * b:LAT * (b + 1)], (LAT, LAT)).T for b in range(3)]

    early[0].wait()
    at_lat, at_weight, at_growth = columns_of(bins_ref[:, :LOCAL]), columns_of(own(LOCAL)), columns_of(own(5 * LOCAL))
    for b in range(3):
        rows = min(LAT, PADDED - LAT * b)
        real = min(LAT, LOCAL - LAT * b)
        to = pl.ds(LAT * b, rows)
        along = cour_ref[pl.ds(LAT * b, real), :]
        if real < rows:
            along = jnp.concatenate([along, jnp.zeros((rows - real, LAT), jnp.float32)], axis=0)
        up, down_by = jnp.maximum(along, 0.0), jnp.minimum(along, 0.0)
        lat = at_lat[b][:rows]
        north, south = jnp.maximum(lat, 0.0), jnp.minimum(lat, 0.0)
        lanes = lax.broadcasted_iota(jnp.int32, (rows, LAT), 1)
        coef[0, to, :] = 1.0 - up + down_by - north + south
        coef[1, to, :] = up
        coef[2, to, :] = -down_by
        coef[3, to, :] = jnp.where(lanes == 0, 0.0, north)
        coef[4, to, :] = jnp.where(lanes == LAT - 1, 0.0, -south)
        coef[5, to, :] = at_weight[b][:rows]
        grow[to, :] = at_growth[b][:rows]

    steep[...] = jnp.zeros_like(steep)
    pad = PADDED - LOCAL
    x[:, pl.ds(LOCAL, pad), :] = jnp.zeros((LON + 2, pad, LAT), jnp.float32)
    for p in range(GROUPS):
        tail[p, :, pl.ds(SIZES[-1] - pad, pad), :] = jnp.zeros((OWN, pad, LAT), jnp.float32)
    packed[pl.ds(0, 2)] = jnp.zeros((2,) + packed.shape[1:], jnp.float32)

    def tile_rows(first):
        return pl.ds(first if isinstance(first, int) else pl.multiple_of(first, 8), 8)

    def tiles_of(start, n, base):
        at = [tile_rows(base + 8 * j) for j in range(n)]
        to = [tile_rows(base - start + 8 * j) for j in range(n)]
        return at, to, [[coef[q, at[j], :] for q in range(6)] for j in range(n)]

    def masked(row, rows):
        return x[row, rows, :] * sea[row]

    def upwind(coefs, low_side, mid, high_side, land):
        c0, cw, ce, cs, cn, _ = coefs
        value = c0 * mid + cw * low_side + ce * high_side
        value = value + cs * pltpu.roll(mid, 1, 1) + cn * pltpu.roll(mid, LAT - 1, 1)
        return value * land

    def inner(start, n, base):
        at, to, coefs = tiles_of(start, n, base)

        def treat(steps, sides, hold):
            stores = []
            for i in steps:
                land, turn, low, over, total = sea[i], source[i], low_ref[i] != 0, cross[i] != 0, steep[i]
                new_hold = []
                for j in range(n):
                    low_side, mid = sides[j]
                    high_side = masked(i + 1, at[j])
                    value = upwind(coefs[j], low_side, mid, high_side, land)
                    total = total + coefs[j][5] * value
                    turned = jnp.take_along_axis(value, turn, axis=1)
                    kept = jnp.where(low, turned, hold[j])
                    stores.append((moved, i - 1, at[j], value))
                    stores.append((packed, i, to[j], kept))
                    new_hold.append(jnp.where(over, turned, kept))
                    sides[j] = (mid, high_side)
                stores.append((steep, i, slice(None), total))
                hold = new_hold
            for ref, i, rows, value in stores:
                ref[i, rows, :] = value
            return sides, hold

        def several(s, carry):
            sides, hold = treat(
                [2 + s * ROWS_AT_ONCE + u for u in range(ROWS_AT_ONCE)], list(carry[0]), list(carry[1])
            )
            return (tuple(sides), tuple(hold))

        sides = tuple((masked(1, at[j]), masked(2, at[j])) for j in range(n))
        hold = tuple(jnp.zeros((8, LAT), jnp.float32) for j in range(n))
        count = (LON - 2) // ROWS_AT_ONCE
        sides, hold = lax.fori_loop(0, count, several, (sides, hold))
        _, hold = treat(list(range(2 + count * ROWS_AT_ONCE, LON)), list(sides), list(hold))
        for j in range(n):
            packed[LON, to[j], :] = hold[j]

    def outer(start, n, base):
        at, to, coefs = tiles_of(start, n, base)
        first_cells = head[0] != 0
        totals = [steep[0], steep[1]]
        stores = []
        for j in range(n):
            turned = []
            for i, row in ((0, LON), (1, 1)):
                value = upwind(coefs[j], masked(row - 1, at[j]), masked(row, at[j]), masked(row + 1, at[j]), sea[row])
                totals[i] = totals[i] + coefs[j][5] * value
                stores.append((moved, row - 1, at[j], value))
                turned.append(jnp.take_along_axis(value, source[i], axis=1))
            stores.append((edge, 0, to[j], jnp.where(first_cells, turned[0], turned[1])))
            stores.append((edge, 1, to[j], turned[1]))
        for ref, i, rows, value in stores:
            ref[i, rows, :] = value
        steep[0], steep[1] = totals

    def landing(c):
        if c == PARTS - 1:
            return tail.at[me]
        return recv.at[:, pl.ds(pl.multiple_of(KSTARTS[c] + me * SIZES[c], 8), SIZES[c]), :]

    def for_all_tiles(treat, start, size):
        odd = 3 * (size // 8 % 2)

        def pair(s, _):
            treat(start, 2, start + s * 16)
            return 0

        lax.fori_loop(0, (size // 8 - odd) // 2, pair, 0)
        if odd:
            treat(start, odd, start + size - 8 * odd)

    sends = {}

    def send(c, half):
        start, size = STARTS[c], SIZES[c]
        rows = min(size, LOCAL - start)
        tiles = pl.ds(HALF * (1 - half), HALF)
        for d in (2, 1, 3):
            copy = pltpu.make_async_remote_copy(
                src_ref=stage.at[d - 1, tiles, pl.ds(start, rows), :],
                dst_ref=landing(c).at[tiles, pl.ds(0, rows), :],
                send_sem=send_sem.at[half, c, d - 1], recv_sem=recv_sem.at[half, c, d - 1],
                device_id=(block, peer(d)), device_id_type=MESH,
            )
            copy.start()
            sends[half, c, d] = copy

    edges = []
    for c in range(PARTS):
        start, size = STARTS[c], SIZES[c]
        loads[c].wait()
        for_all_tiles(inner, start, size)
        if c == 0:
            copy_last.wait()
        mine = landing(c)
        for d in (2, 1, 3, 0):
            to = peer(d)
            values = [
                packed[last[0, to * OWN + k], pl.ds(0, size), :] for k in range(OWN)
            ]
            for k in range(OWN):
                if d == 0:
                    mine[k] = values[k]
                else:
                    stage[d - 1, k, pl.ds(start, size), :] = values[k]
        if c == 0:
            pl.semaphore_wait(barrier, 5)
            for slot, row, into, to in ((0, LON - 1, 0, east), (1, 0, LON + 1, west)):
                for k, src, dst in (
                    (slot, spec_ref.at[row], x.at[into, pl.ds(0, LOCAL), :]),
                    (2 + slot, sea.at[row + 1], sea.at[into]),
                ):
                    copy = pltpu.make_async_remote_copy(
                        src_ref=src, dst_ref=dst, send_sem=halo_send.at[k], recv_sem=halo_recv.at[k],
                        device_id=(to, me), device_id_type=MESH,
                    )
                    copy.start()
                    edges.append(copy)
        send(c, 0)

    for copy in edges:
        copy.wait()
    for c in range(PARTS):
        start, size = STARTS[c], SIZES[c]
        for_all_tiles(outer, start, size)
        for d in (2, 1, 3, 0):
            here = jnp.where(peer(d) == 0, 1, 0)
            share = landing(c) if d == 0 else stage.at[d - 1, :, pl.ds(start, size), :]
            for k in range(2):
                old = share[k]
                use = jnp.broadcast_to((head[1 + k] * here)[:1, :], (size, LAT)) != 0
                new = jnp.where(use, edge[k, pl.ds(0, size), :], old)
                share[k] = new
        send(c, 1)

    sums[0] = jnp.sum(steep[...], axis=1)
    sum_copies = []
    for d in (1, 2, 3):
        copy = pltpu.make_async_remote_copy(
            src_ref=sums.at[0], dst_ref=sums.at[d], send_sem=sum_send.at[d - 1], recv_sem=sum_recv.at[d - 1],
            device_id=(block, peer(d)), device_id_type=MESH,
        )
        copy.start()
        sum_copies.append(copy)

    exact = functools.partial(jnp.dot, precision=lax.Precision.HIGHEST, preferred_element_type=jnp.float32)
    for copy in early[1:]:
        copy.wait()
    fcols[...] = exact(fmix_ref[...], fcol_ref[...])
    spread = time_step * exact(dmix_ref[...], dcol_ref[...])
    for j in range(4):
        dcols[pl.ds(j * ND, ND), :] = spread

    def matrix_rows(p, _):
        for g, (size, count) in enumerate(((144, 4), (144, 4), (48, 1))):
            for first in range(0, KTOTAL - 255, 256):
                width = 256 if first + 512 <= KTOTAL else KTOTAL - first
                cols = pl.ds(first, width)
                index = lax.broadcasted_iota(jnp.int32, (size, width), 0)
                rows = [fcols[pl.ds(p * 9 + 4 * g + j, 1), cols] for j in range(count)]
                if count == 1:
                    factor = jnp.where(index < ND, rows[0], 0.0)
                else:
                    factor = jnp.where(
                        index < 2 * ND,
                        jnp.where(index < ND, rows[0], rows[1]),
                        jnp.where(index < 3 * ND, rows[2], rows[3]),
                    )
                value = factor * dcols[pl.ds(0, size), cols]
                high = value.astype(jnp.bfloat16)
                low = (value - high.astype(jnp.float32)).astype(jnp.bfloat16)
                at = pl.ds(144 * g, size)
                w_hi[p, at, cols] = high
                w_lo[p, at, cols] = low
        return 0

    lax.fori_loop(0, GROUPS, matrix_rows, 0)

    def arrive(half):
        for c in range(PARTS):
            for d in (1, 2, 3):
                sends[half, c, d].wait_recv()

    def mix(half):
        for s in range(HALF // 2):
            k = HALF * (1 - half) + 2 * s
            for c in range(PARTS):
                rows = pl.ds(KSTARTS[c], GROUPS * SIZES[c])
                if c == PARTS - 1:
                    both = [jnp.concatenate([tail[p, k + u] for p in range(GROUPS)], axis=0) for u in range(2)]
                else:
                    both = [recv[k + u, rows, :] for u in range(2)]
                value = jnp.concatenate(both, axis=1)
                high = value.astype(jnp.bfloat16)
                f_hi[rows, :] = high
                f_lo[rows, :] = (value - high.astype(jnp.float32)).astype(jnp.bfloat16)

            def rows_of(p, _, k=k):
                value = dot(w_hi[p], f_hi[...]) + dot(w_lo[p], f_hi[...]) + dot(w_hi[p], f_lo[...])
                acc[p, k] = value[:, :LAT]
                acc[p, k + 1] = value[:, LAT:]
                return 0

            lax.fori_loop(0, GROUPS, rows_of, 0)

    backs = []

    def send_back(half, d):
        p = peer(d)
        src = acc.at[p, pl.ds(HALF * (1 - half), HALF), pl.ds(0, LOCAL), :]
        tiles = pl.ds(me * OWN + HALF * (1 - half), HALF)
        if d == 0:
            copy = pltpu.make_async_copy(src, mixed_ref.at[tiles], own_sem.at[half])
        else:
            copy = pltpu.make_async_remote_copy(
                src_ref=src, dst_ref=mixed_ref.at[tiles],
                send_sem=back_send.at[half, d - 1], recv_sem=back_recv.at[half, d - 1],
                device_id=(block, p), device_id_type=MESH,
            )
        copy.start()
        backs.append(copy)

    arrive(0)
    mix(0)
    send_back(0, 2)
    arrive(1)
    for d in (1, 3, 0):
        send_back(0, d)
    mix(1)
    for d in (2, 1, 3, 0):
        send_back(1, d)

    for copy in sum_copies:
        copy.wait()
    whole = (sums[0] + sums[1]) + (sums[2] + sums[3])
    whole = dissipation * whole / (1.0 + whole)
    for i in range(LON):
        damp[i] = jnp.broadcast_to(whole[i:i + 1, :], (8, LAT))

    def add_own(i, row):
        keep = time_step * live_ref[i]
        gusts, damps = gust[i], damp[i]
        values = []
        for t in range(PADDED // 8):
            value = moved[row, pl.ds(8 * t, 8), :]
            values.append(value + keep * (value * (grow[pl.ds(8 * t, 8), :] * gusts - damps)))
        for t in range(PADDED // 8):
            moved[row, pl.ds(8 * t, 8), :] = values[t]

    def rows_own(i, _):
        add_own(i, i - 1)
        return 0

    lax.fori_loop(1, LON, rows_own, 0)
    add_own(0, LON - 1)
    store = pltpu.make_async_copy(moved.at[:, pl.ds(0, LOCAL), :], moved_ref, out_sem)
    store.start()
    for copy in late:
        copy.wait()
    store.wait()
    for copy in sends.values():
        copy.wait_send()
    for copy in backs:
        copy.wait()


def finish_kernel(first_ref, moved_ref, mixed_ref, live_ref, low_ref, place_ref, out_ref):
    tiles = moved_ref.shape[1] // 8

    def treat(todo):
        stores = []
        for i, row in todo:
            first = first_ref[i, 0]
            after = jnp.minimum(first + 1, TILES - 1)
            low, place, live = low_ref[i] != 0, place_ref[i], live_ref[i] != 0.0
            for j in range(tiles):
                at = pl.ds(8 * j, 8)
                joined = jnp.where(low, mixed_ref[first, at, :], mixed_ref[after, at, :])
                term = jnp.take_along_axis(joined, place, axis=1)
                stores.append((row, at, moved_ref[row, at, :] + jnp.where(live, term, 0.0)))
        for row, at, value in stores:
            out_ref[row, at, :] = value

    def several(s, _):
        treat([(s * 4 + u + 1, s * 4 + u) for u in range(4)])
        return 0

    lax.fori_loop(0, (LON - 1) // 4, several, 0)
    treat([(0, LON - 1)])


def on_device(
    spectrum, sea_mask, cour_lon, cour_lat, wind, growth_rate, band_weight, freq_mix, dir_mix, routes, counts
):
    spec = jnp.transpose(spectrum, (1, 0, 2))
    fcol, dcol = column_maps()
    f32, bf16, i32 = jnp.float32, jnp.bfloat16, jnp.int32
    vmem = pl.BlockSpec(memory_space=pltpu.VMEM)
    hbm = pl.BlockSpec(memory_space=pl.ANY)
    smem = pl.BlockSpec(memory_space=pltpu.SMEM)
    dma = pltpu.SemaphoreType.DMA
    wide = (LON, 8, LAT)
    moved, mixed, live, low, place, first = pl.pallas_call(
        exchange_kernel,
        out_shape=(
            jax.ShapeDtypeStruct((LON, LOCAL, LAT), f32),
            jax.ShapeDtypeStruct((TILES, LOCAL, LAT), f32),
            jax.ShapeDtypeStruct(wide, f32),
            jax.ShapeDtypeStruct(wide, i32),
            jax.ShapeDtypeStruct(wide, i32),
            jax.ShapeDtypeStruct((LON + 3, LAT), i32),
        ),
        in_specs=[hbm, vmem, hbm] + [vmem] * 4 + [hbm, hbm],
        out_specs=(hbm,) * 6,
        scratch_shapes=[
            pltpu.VMEM((LOCAL, LAT), f32),
            pltpu.VMEM((NF, KTOTAL), f32),
            pltpu.VMEM((ND, KTOTAL), f32),
            pltpu.VMEM(wide, f32),
            pltpu.VMEM(wide, i32),
            pltpu.VMEM(wide, i32),
            pltpu.VMEM((LON + 3, LAT), i32),
            pltpu.VMEM((LON + 2, PADDED, LAT), f32),
            pltpu.VMEM((LON, PADDED, LAT), f32),
            pltpu.VMEM((LON + 2, 8, LAT), f32),
            pltpu.VMEM(wide, f32),
            pltpu.VMEM(wide, f32),
            pltpu.VMEM(wide, i32),
            pltpu.VMEM(wide, i32),
            pltpu.VMEM((3, 8, LAT), i32),
            pltpu.VMEM((LON + 3, LAT), f32),
            pltpu.VMEM((8, LAT), i32),
            pltpu.SMEM((8, LAT), i32),
            pltpu.VMEM((6, PADDED, LAT), f32),
            pltpu.VMEM((PADDED, LAT), f32),
            pltpu.VMEM((LON + 1, max(SIZES), LAT), f32),
            pltpu.VMEM((2, max(SIZES), LAT), f32),
            pltpu.VMEM((GROUPS - 1, OWN, PADDED, LAT), f32),
            pltpu.VMEM((OWN, KSTARTS[-1], LAT), f32),
            pltpu.VMEM((GROUPS, OWN, SIZES[-1], LAT), f32),
            pltpu.VMEM((GROUPS, OWN, MROWS, LAT), f32),
            pltpu.VMEM((GROUPS, MROWS, KTOTAL), bf16),
            pltpu.VMEM((GROUPS, MROWS, KTOTAL), bf16),
            pltpu.VMEM((KTOTAL, 256), bf16),
            pltpu.VMEM((KTOTAL, 256), bf16),
            pltpu.VMEM((NF, KTOTAL), f32),
            pltpu.VMEM((4 * ND, KTOTAL), f32),
            pltpu.VMEM(wide, f32),
            pltpu.VMEM((GROUPS, LON, LAT), f32),
            dma((PARTS,)), dma((4,)), dma((4,)), dma((2, PARTS, 3)), dma((2, PARTS, 3)),
            dma((2, 3)), dma((2, 3)), dma((3,)), dma((3,)), dma((2,)), dma, dma,
            dma((3,)), dma((4,)),
        ],
        compiler_params=pltpu.CompilerParams(
            collective_id=0, has_side_effects=True, vmem_limit_bytes=56 << 20
        ),
    )(
        spec, sea_mask, cour_lon, wind,
        jnp.concatenate([cour_lat, band_weight, growth_rate]).reshape(1, -1), freq_mix, dir_mix, jnp.asarray(fcol), jnp.asarray(dcol),
    )
    step = 88
    whole = pl.BlockSpec(wide, lambda c: (0, 0, 0))
    out = pl.pallas_call(
        finish_kernel,
        out_shape=jax.ShapeDtypeStruct((LON, LOCAL, LAT), f32),
        grid=(pl.cdiv(LOCAL, step),),
        in_specs=[
            smem,
            pl.BlockSpec((LON, step, LAT), lambda c: (0, c, 0)),
            pl.BlockSpec((TILES, step, LAT), lambda c: (0, c, 0)),
            whole, whole, whole,
        ],
        out_specs=pl.BlockSpec((LON, step, LAT), lambda c: (0, c, 0)),
        compiler_params=pltpu.CompilerParams(vmem_limit_bytes=58 << 20),
    )(first, moved, mixed, live, low, place)
    return jnp.transpose(out, (1, 0, 2))


def solution(mesh):
    placed = (
        P("bin", "lon", None),
        P("lon", None),
        P("bin", None),
        P("bin"),
        P("lon", None),
        P(),
        P(),
        P(),
        P(),
        P("lon", None, None),
        P("lon", None),
    )
    return jax.shard_map(
        on_device, mesh=mesh, in_specs=placed, out_specs=P("bin", "lon", None), check_vma=False
    )
```

```python
import functools

import jax
import jax.numpy as jnp
import numpy as np
from jax import lax
from jax.experimental import pallas as pl
from jax.experimental.pallas import tpu as pltpu
from jax.sharding import PartitionSpec as P

MESH = pl.DeviceIdType.MESH
dissipation = 0.5
time_step = 0.5
NF, ND = 36, 36
LON, LAT = 45, 128
GROUPS = 4
LOCAL = 324
PADDED = 328
CELLS = 4096
SHARE = CELLS // GROUPS
TILES = CELLS // LAT
SIZES = (16, 32, 48, 96, 136)
STARTS = (0, 16, 48, 96, 192)
PARTS = len(SIZES)
KSTARTS = tuple(GROUPS * s for s in STARTS)
KTOTAL = GROUPS * PADDED
MROWS = 336
OWN = SHARE // LAT
HALF = OWN // 2
ROWS_AT_ONCE = 10


def column_maps():
    freq = np.zeros((NF, KTOTAL), np.float32)
    direction = np.zeros((ND, KTOTAL), np.float32)
    at = 0
    for start, size in zip(STARTS, SIZES):
        for p in range(GROUPS):
            for b in range(start, start + size):
                if b < LOCAL:
                    k = p * LOCAL + b
                    freq[k // ND, at] = 1.0
                    direction[k % ND, at] = 1.0
                at += 1
    return freq, direction


def exchange_kernel(
    spec_ref, mask_ref, cour_hbm, wind_ref, lat_ref, weight_ref, growth_ref, fmix_ref, dmix_ref, fcol_hbm, dcol_hbm,
    moved_ref, mixed_ref, live_out, low_out, place_out, first_out,
    cour_ref, fcol_ref, dcol_ref, live_ref, low_ref, place_ref, first_ref,
    x, moved, sea, gust, damp, source, cross, head, order, last_rows, last, coef, grow, packed, edge, stage, recv, tail, acc,
    w_hi, w_lo, f_hi, f_lo, fcols, dcols, steep, sums,
    in_sem, halo_send, halo_recv, send_sem, recv_sem, back_send, back_recv, sum_send, sum_recv, own_sem, last_sem, out_sem,
    early_sem, late_sem,
):
    me = lax.axis_index("bin")
    block = lax.axis_index("lon")
    blocks = lax.axis_size("lon")
    west = lax.rem(block + blocks - 1, blocks)
    east = lax.rem(block + 1, blocks)

    def peer(d):
        return lax.rem(me + d, GROUPS)

    barrier = pltpu.get_barrier_semaphore()
    for d in (1, 2, 3):
        pl.semaphore_signal(barrier, inc=1, device_id=(block, peer(d)), device_id_type=MESH)
    pl.semaphore_signal(barrier, inc=1, device_id=(west, me), device_id_type=MESH)
    pl.semaphore_signal(barrier, inc=1, device_id=(east, me), device_id_type=MESH)

    early = [
        pltpu.make_async_copy(src, dst, early_sem.at[q])
        for q, (src, dst) in enumerate(((cour_hbm, cour_ref), (fcol_hbm, fcol_ref), (dcol_hbm, dcol_ref)))
    ]
    early[0].start()

    loads = []
    for c in range(PARTS):
        rows = min(SIZES[c], LOCAL - STARTS[c])
        copy = pltpu.make_async_copy(
            spec_ref.at[:, pl.ds(STARTS[c], rows), :],
            x.at[pl.ds(1, LON), pl.ds(STARTS[c], rows), :],
            in_sem.at[c],
        )
        copy.start()
        loads.append(copy)

    for copy in early[1:]:
        copy.start()

    flags = mask_ref[...].astype(jnp.float32)
    for r in range(LON):
        wide = jnp.broadcast_to(flags[r:r + 1, :], (8, LAT))
        sea[r + 1] = wide
        live_ref[(r + 1) % LON] = wide
    order[pl.ds(0, 1), :] = flags[LON - 1:, :]
    order[pl.ds(1, LON - 1), :] = flags[:LON - 1, :]
    order[pl.ds(LON, 3), :] = jnp.zeros((3, LAT), jnp.float32)

    dot = functools.partial(jnp.dot, preferred_element_type=jnp.float32)
    steps = LON + 3
    here = order[...]
    down = lax.broadcasted_iota(jnp.int32, (LAT, LAT), 0)
    across = lax.broadcasted_iota(jnp.int32, (LAT, LAT), 1)
    rank = dot(here, (down <= across).astype(jnp.float32))
    number = dot(here, jnp.ones((LAT, LAT), jnp.float32))
    before = lax.broadcasted_iota(jnp.int32, (steps, steps), 0) > lax.broadcasted_iota(jnp.int32, (steps, steps), 1)
    offset = dot(before.astype(jnp.float32), number).astype(jnp.int32)
    lane = lax.broadcasted_iota(jnp.int32, (steps, LAT), 1)
    step_of = lax.broadcasted_iota(jnp.int32, (steps, LAT), 0)
    reached = jnp.where((offset <= lane * LAT + (LAT - 1)) & (step_of <= LON), 1, 0)
    last_rows[...] = jnp.broadcast_to(jnp.sum(reached, axis=0, keepdims=True) - 1, (8, LAT))
    copy_last = pltpu.make_async_copy(last_rows, last, last_sem)
    copy_last.start()
    first_ref[...] = jnp.minimum(offset // LAT, TILES - 1)
    shift = offset % LAT
    for t in range(steps // 8):
        some = slice(8 * t, 8 * t + 8)
        ranks, moved_by = rank[some], shift[some]
        lanes = lane[some]
        wanted = ((lanes - moved_by + LAT) % LAT).astype(jnp.float32)
        position = jnp.zeros((8, LAT), jnp.int32)
        for half in (64, 32, 16, 8, 4, 2, 1):
            probe = jnp.take_along_axis(ranks, position + (half - 1), axis=1)
            position = jnp.where(probe <= wanted, position + half, position)
        low = (lanes >= moved_by).astype(jnp.int32)
        over = (moved_by.astype(jnp.float32) + number[some] >= LAT).astype(jnp.int32)
        place = (moved_by + ranks.astype(jnp.int32) + (LAT - 1)) % LAT
        for u in range(8):
            i = 8 * t + u
            if i < LON:
                for ref, value in ((source, position), (low_ref, low), (cross, over), (place_ref, place)):
                    ref[i] = jnp.broadcast_to(value[u:u + 1, :], (8, LAT))
                r = (i - 1) % LON
                gust[i] = jnp.broadcast_to(wind_ref[r:r + 1, :], (8, LAT))

    late = [
        pltpu.make_async_copy(src, dst, late_sem.at[q])
        for q, (src, dst) in enumerate(
            ((live_ref, live_out), (low_ref, low_out), (place_ref, place_out), (first_ref, first_out))
        )
    ]
    for copy in late:
        copy.start()

    lanes = lane[:8]
    first_cells, edge_cells = offset[1:2, :], offset[2:3, :]
    head[0] = (lanes < first_cells).astype(jnp.int32)
    head[1] = (lanes < edge_cells).astype(jnp.int32)
    head[2] = (lanes + LAT < edge_cells).astype(jnp.int32)

    def own(ref):
        row = ref[...].reshape(1, GROUPS * LOCAL)
        part = [row[:, LOCAL * p:LOCAL * (p + 1)] for p in range(GROUPS)]
        return jnp.where(me < 2, jnp.where(me == 0, part[0], part[1]), jnp.where(me == 2, part[2], part[3]))

    def columns_of(row):
        row = jnp.concatenate([row, jnp.zeros((1, 3 * LAT - LOCAL), jnp.float32)], axis=1)
        return [jnp.broadcast_to(row[:, LAT * b:LAT * (b + 1)], (LAT, LAT)).T for b in range(3)]

    early[0].wait()
    at_lat, at_weight, at_growth = columns_of(lat_ref[...].reshape(1, LOCAL)), columns_of(own(weight_ref)), columns_of(own(growth_ref))
    for b in range(3):
        rows = min(LAT, PADDED - LAT * b)
        real = min(LAT, LOCAL - LAT * b)
        to = pl.ds(LAT * b, rows)
        along = cour_ref[pl.ds(LAT * b, real), :]
        if real < rows:
            along = jnp.concatenate([along, jnp.zeros((rows - real, LAT), jnp.float32)], axis=0)
        up, down_by = jnp.maximum(along, 0.0), jnp.minimum(along, 0.0)
        lat = at_lat[b][:rows]
        north, south = jnp.maximum(lat, 0.0), jnp.minimum(lat, 0.0)
        lanes = lax.broadcasted_iota(jnp.int32, (rows, LAT), 1)
        coef[0, to, :] = 1.0 - up + down_by - north + south
        coef[1, to, :] = up
        coef[2, to, :] = -down_by
        coef[3, to, :] = jnp.where(lanes == 0, 0.0, north)
        coef[4, to, :] = jnp.where(lanes == LAT - 1, 0.0, -south)
        coef[5, to, :] = at_weight[b][:rows]
        grow[to, :] = at_growth[b][:rows]

    steep[...] = jnp.zeros_like(steep)
    pad = PADDED - LOCAL
    x[:, pl.ds(LOCAL, pad), :] = jnp.zeros((LON + 2, pad, LAT), jnp.float32)
    for p in range(GROUPS):
        tail[p, :, pl.ds(SIZES[-1] - pad, pad), :] = jnp.zeros((OWN, pad, LAT), jnp.float32)
    packed[pl.ds(0, 2)] = jnp.zeros((2,) + packed.shape[1:], jnp.float32)

    def tile_rows(first):
        return pl.ds(first if isinstance(first, int) else pl.multiple_of(first, 8), 8)

    def tiles_of(start, n, base):
        at = [tile_rows(base + 8 * j) for j in range(n)]
        to = [tile_rows(base - start + 8 * j) for j in range(n)]
        return at, to, [[coef[q, at[j], :] for q in range(6)] for j in range(n)]

    def masked(row, rows):
        return x[row, rows, :] * sea[row]

    def upwind(coefs, low_side, mid, high_side, land):
        c0, cw, ce, cs, cn, _ = coefs
        value = c0 * mid + cw * low_side + ce * high_side
        value = value + cs * pltpu.roll(mid, 1, 1) + cn * pltpu.roll(mid, LAT - 1, 1)
        return value * land

    def inner(start, n, base):
        at, to, coefs = tiles_of(start, n, base)

        def treat(steps, sides, hold):
            stores = []
            for i in steps:
                land, turn, low, over, total = sea[i], source[i], low_ref[i] != 0, cross[i] != 0, steep[i]
                new_hold = []
                for j in range(n):
                    low_side, mid = sides[j]
                    high_side = masked(i + 1, at[j])
                    value = upwind(coefs[j], low_side, mid, high_side, land)
                    total = total + coefs[j][5] * value
                    turned = jnp.take_along_axis(value, turn, axis=1)
                    kept = jnp.where(low, turned, hold[j])
                    stores.append((moved, i - 1, at[j], value))
                    stores.append((packed, i, to[j], kept))
                    new_hold.append(jnp.where(over, turned, kept))
                    sides[j] = (mid, high_side)
                stores.append((steep, i, slice(None), total))
                hold = new_hold
            for ref, i, rows, value in stores:
                ref[i, rows, :] = value
            return sides, hold

        def several(s, carry):
            sides, hold = treat(
                [2 + s * ROWS_AT_ONCE + u for u in range(ROWS_AT_ONCE)], list(carry[0]), list(carry[1])
            )
            return (tuple(sides), tuple(hold))

        sides = tuple((masked(1, at[j]), masked(2, at[j])) for j in range(n))
        hold = tuple(jnp.zeros((8, LAT), jnp.float32) for j in range(n))
        count = (LON - 2) // ROWS_AT_ONCE
        sides, hold = lax.fori_loop(0, count, several, (sides, hold))
        _, hold = treat(list(range(2 + count * ROWS_AT_ONCE, LON)), list(sides), list(hold))
        for j in range(n):
            packed[LON, to[j], :] = hold[j]

    def outer(start, n, base):
        at, to, coefs = tiles_of(start, n, base)
        first_cells = head[0] != 0
        totals = [steep[0], steep[1]]
        stores = []
        for j in range(n):
            turned = []
            for i, row in ((0, LON), (1, 1)):
                value = upwind(coefs[j], masked(row - 1, at[j]), masked(row, at[j]), masked(row + 1, at[j]), sea[row])
                totals[i] = totals[i] + coefs[j][5] * value
                stores.append((moved, row - 1, at[j], value))
                turned.append(jnp.take_along_axis(value, source[i], axis=1))
            stores.append((edge, 0, to[j], jnp.where(first_cells, turned[0], turned[1])))
            stores.append((edge, 1, to[j], turned[1]))
        for ref, i, rows, value in stores:
            ref[i, rows, :] = value
        steep[0], steep[1] = totals

    def landing(c):
        if c == PARTS - 1:
            return tail.at[me]
        return recv.at[:, pl.ds(pl.multiple_of(KSTARTS[c] + me * SIZES[c], 8), SIZES[c]), :]

    def for_all_tiles(treat, start, size):
        odd = 3 * (size // 8 % 2)

        def pair(s, _):
            treat(start, 2, start + s * 16)
            return 0

        lax.fori_loop(0, (size // 8 - odd) // 2, pair, 0)
        if odd:
            treat(start, odd, start + size - 8 * odd)

    sends = {}

    def send(c, half):
        start, size = STARTS[c], SIZES[c]
        rows = min(size, LOCAL - start)
        tiles = pl.ds(HALF * (1 - half), HALF)
        for d in (2, 1, 3):
            copy = pltpu.make_async_remote_copy(
                src_ref=stage.at[d - 1, tiles, pl.ds(start, rows), :],
                dst_ref=landing(c).at[tiles, pl.ds(0, rows), :],
                send_sem=send_sem.at[half, c, d - 1], recv_sem=recv_sem.at[half, c, d - 1],
                device_id=(block, peer(d)), device_id_type=MESH,
            )
            copy.start()
            sends[half, c, d] = copy

    edges = []
    for c in range(PARTS):
        start, size = STARTS[c], SIZES[c]
        loads[c].wait()
        for_all_tiles(inner, start, size)
        if c == 0:
            copy_last.wait()
        mine = landing(c)
        for d in (2, 1, 3, 0):
            to = peer(d)
            values = [
                packed[last[0, to * OWN + k], pl.ds(0, size), :] for k in range(OWN)
            ]
            for k in range(OWN):
                if d == 0:
                    mine[k] = values[k]
                else:
                    stage[d - 1, k, pl.ds(start, size), :] = values[k]
        if c == 0:
            pl.semaphore_wait(barrier, 5)
            for slot, row, into, to in ((0, LON - 1, 0, east), (1, 0, LON + 1, west)):
                for k, src, dst in (
                    (slot, spec_ref.at[row], x.at[into, pl.ds(0, LOCAL), :]),
                    (2 + slot, sea.at[row + 1], sea.at[into]),
                ):
                    copy = pltpu.make_async_remote_copy(
                        src_ref=src, dst_ref=dst, send_sem=halo_send.at[k], recv_sem=halo_recv.at[k],
                        device_id=(to, me), device_id_type=MESH,
                    )
                    copy.start()
                    edges.append(copy)
        send(c, 0)

    for copy in edges:
        copy.wait()
    for c in range(PARTS):
        start, size = STARTS[c], SIZES[c]
        for_all_tiles(outer, start, size)
        for d in (2, 1, 3, 0):
            here = jnp.where(peer(d) == 0, 1, 0)
            share = landing(c) if d == 0 else stage.at[d - 1, :, pl.ds(start, size), :]
            for k in range(2):
                old = share[k]
                use = jnp.broadcast_to((head[1 + k] * here)[:1, :], (size, LAT)) != 0
                new = jnp.where(use, edge[k, pl.ds(0, size), :], old)
                share[k] = new
        send(c, 1)

    sums[0] = jnp.sum(steep[...], axis=1)
    sum_copies = []
    for d in (1, 2, 3):
        copy = pltpu.make_async_remote_copy(
            src_ref=sums.at[0], dst_ref=sums.at[d], send_sem=sum_send.at[d - 1], recv_sem=sum_recv.at[d - 1],
            device_id=(block, peer(d)), device_id_type=MESH,
        )
        copy.start()
        sum_copies.append(copy)

    exact = functools.partial(jnp.dot, precision=lax.Precision.HIGHEST, preferred_element_type=jnp.float32)
    for copy in early[1:]:
        copy.wait()
    fcols[...] = exact(fmix_ref[...], fcol_ref[...])
    spread = time_step * exact(dmix_ref[...], dcol_ref[...])
    for j in range(4):
        dcols[pl.ds(j * ND, ND), :] = spread

    def matrix_rows(p, _):
        for g, (size, count) in enumerate(((144, 4), (144, 4), (48, 1))):
            for first in range(0, KTOTAL - 255, 256):
                width = 256 if first + 512 <= KTOTAL else KTOTAL - first
                cols = pl.ds(first, width)
                index = lax.broadcasted_iota(jnp.int32, (size, width), 0)
                rows = [fcols[pl.ds(p * 9 + 4 * g + j, 1), cols] for j in range(count)]
                if count == 1:
                    factor = jnp.where(index < ND, rows[0], 0.0)
                else:
                    factor = jnp.where(
                        index < 2 * ND,
                        jnp.where(index < ND, rows[0], rows[1]),
                        jnp.where(index < 3 * ND, rows[2], rows[3]),
                    )
                value = factor * dcols[pl.ds(0, size), cols]
                high = value.astype(jnp.bfloat16)
                low = (value - high.astype(jnp.float32)).astype(jnp.bfloat16)
                at = pl.ds(144 * g, size)
                w_hi[p, at, cols] = high
                w_lo[p, at, cols] = low
        return 0

    lax.fori_loop(0, GROUPS, matrix_rows, 0)

    def arrive(half):
        for c in range(PARTS):
            for d in (1, 2, 3):
                sends[half, c, d].wait_recv()

    def mix(half):
        for s in range(HALF // 2):
            k = HALF * (1 - half) + 2 * s
            for c in range(PARTS):
                rows = pl.ds(KSTARTS[c], GROUPS * SIZES[c])
                if c == PARTS - 1:
                    both = [jnp.concatenate([tail[p, k + u] for p in range(GROUPS)], axis=0) for u in range(2)]
                else:
                    both = [recv[k + u, rows, :] for u in range(2)]
                value = jnp.concatenate(both, axis=1)
                high = value.astype(jnp.bfloat16)
                f_hi[rows, :] = high
                f_lo[rows, :] = (value - high.astype(jnp.float32)).astype(jnp.bfloat16)

            def rows_of(p, _, k=k):
                value = dot(w_hi[p], f_hi[...]) + dot(w_lo[p], f_hi[...]) + dot(w_hi[p], f_lo[...])
                acc[p, k] = value[:, :LAT]
                acc[p, k + 1] = value[:, LAT:]
                return 0

            lax.fori_loop(0, GROUPS, rows_of, 0)

    backs = []

    def send_back(half, d):
        p = peer(d)
        src = acc.at[p, pl.ds(HALF * (1 - half), HALF), pl.ds(0, LOCAL), :]
        tiles = pl.ds(me * OWN + HALF * (1 - half), HALF)
        if d == 0:
            copy = pltpu.make_async_copy(src, mixed_ref.at[tiles], own_sem.at[half])
        else:
            copy = pltpu.make_async_remote_copy(
                src_ref=src, dst_ref=mixed_ref.at[tiles],
                send_sem=back_send.at[half, d - 1], recv_sem=back_recv.at[half, d - 1],
                device_id=(block, p), device_id_type=MESH,
            )
        copy.start()
        backs.append(copy)

    arrive(0)
    mix(0)
    send_back(0, 2)
    arrive(1)
    for d in (1, 3, 0):
        send_back(0, d)
    mix(1)
    for d in (2, 1, 3, 0):
        send_back(1, d)

    for copy in sum_copies:
        copy.wait()
    whole = (sums[0] + sums[1]) + (sums[2] + sums[3])
    whole = dissipation * whole / (1.0 + whole)
    for i in range(LON):
        damp[i] = jnp.broadcast_to(whole[i:i + 1, :], (8, LAT))

    def add_own(i, row):
        keep = time_step * live_ref[i]
        gusts, damps = gust[i], damp[i]
        values = []
        for t in range(PADDED // 8):
            value = moved[row, pl.ds(8 * t, 8), :]
            values.append(value + keep * (value * (grow[pl.ds(8 * t, 8), :] * gusts - damps)))
        for t in range(PADDED // 8):
            moved[row, pl.ds(8 * t, 8), :] = values[t]

    def rows_own(i, _):
        add_own(i, i - 1)
        return 0

    lax.fori_loop(1, LON, rows_own, 0)
    add_own(0, LON - 1)
    store = pltpu.make_async_copy(moved.at[:, pl.ds(0, LOCAL), :], moved_ref, out_sem)
    store.start()
    for copy in late:
        copy.wait()
    store.wait()
    for copy in sends.values():
        copy.wait_send()
    for copy in backs:
        copy.wait()


def finish_kernel(first_ref, moved_ref, mixed_ref, live_ref, low_ref, place_ref, out_ref):
    tiles = moved_ref.shape[1] // 8

    def treat(todo):
        stores = []
        for i, row in todo:
            first = first_ref[i, 0]
            after = jnp.minimum(first + 1, TILES - 1)
            low, place, live = low_ref[i] != 0, place_ref[i], live_ref[i] != 0.0
            for j in range(tiles):
                at = pl.ds(8 * j, 8)
                joined = jnp.where(low, mixed_ref[first, at, :], mixed_ref[after, at, :])
                term = jnp.take_along_axis(joined, place, axis=1)
                stores.append((row, at, moved_ref[row, at, :] + jnp.where(live, term, 0.0)))
        for row, at, value in stores:
            out_ref[row, at, :] = value

    def several(s, _):
        treat([(s * 11 + u + 1, s * 11 + u) for u in range(11)])
        return 0

    lax.fori_loop(0, (LON - 1) // 11, several, 0)
    treat([(0, LON - 1)])


def on_device(
    spectrum, sea_mask, cour_lon, cour_lat, wind, growth_rate, band_weight, freq_mix, dir_mix, routes, counts
):
    spec = jnp.transpose(spectrum, (1, 0, 2))
    fcol, dcol = column_maps()
    f32, bf16, i32 = jnp.float32, jnp.bfloat16, jnp.int32
    vmem = pl.BlockSpec(memory_space=pltpu.VMEM)
    hbm = pl.BlockSpec(memory_space=pl.ANY)
    smem = pl.BlockSpec(memory_space=pltpu.SMEM)
    dma = pltpu.SemaphoreType.DMA
    wide = (LON, 8, LAT)
    moved, mixed, live, low, place, first = pl.pallas_call(
        exchange_kernel,
        out_shape=(
            jax.ShapeDtypeStruct((LON, LOCAL, LAT), f32),
            jax.ShapeDtypeStruct((TILES, LOCAL, LAT), f32),
            jax.ShapeDtypeStruct(wide, f32),
            jax.ShapeDtypeStruct(wide, i32),
            jax.ShapeDtypeStruct(wide, i32),
            jax.ShapeDtypeStruct((LON + 3, LAT), i32),
        ),
        in_specs=[hbm, vmem, hbm] + [vmem] * 6 + [hbm, hbm],
        out_specs=(hbm,) * 6,
        scratch_shapes=[
            pltpu.VMEM((LOCAL, LAT), f32),
            pltpu.VMEM((NF, KTOTAL), f32),
            pltpu.VMEM((ND, KTOTAL), f32),
            pltpu.VMEM(wide, f32),
            pltpu.VMEM(wide, i32),
            pltpu.VMEM(wide, i32),
            pltpu.VMEM((LON + 3, LAT), i32),
            pltpu.VMEM((LON + 2, PADDED, LAT), f32),
            pltpu.VMEM((LON, PADDED, LAT), f32),
            pltpu.VMEM((LON + 2, 8, LAT), f32),
            pltpu.VMEM(wide, f32),
            pltpu.VMEM(wide, f32),
            pltpu.VMEM(wide, i32),
            pltpu.VMEM(wide, i32),
            pltpu.VMEM((3, 8, LAT), i32),
            pltpu.VMEM((LON + 3, LAT), f32),
            pltpu.VMEM((8, LAT), i32),
            pltpu.SMEM((8, LAT), i32),
            pltpu.VMEM((6, PADDED, LAT), f32),
            pltpu.VMEM((PADDED, LAT), f32),
            pltpu.VMEM((LON + 1, max(SIZES), LAT), f32),
            pltpu.VMEM((2, max(SIZES), LAT), f32),
            pltpu.VMEM((GROUPS - 1, OWN, PADDED, LAT), f32),
            pltpu.VMEM((OWN, KSTARTS[-1], LAT), f32),
            pltpu.VMEM((GROUPS, OWN, SIZES[-1], LAT), f32),
            pltpu.VMEM((GROUPS, OWN, MROWS, LAT), f32),
            pltpu.VMEM((GROUPS, MROWS, KTOTAL), bf16),
            pltpu.VMEM((GROUPS, MROWS, KTOTAL), bf16),
            pltpu.VMEM((KTOTAL, 256), bf16),
            pltpu.VMEM((KTOTAL, 256), bf16),
            pltpu.VMEM((NF, KTOTAL), f32),
            pltpu.VMEM((4 * ND, KTOTAL), f32),
            pltpu.VMEM(wide, f32),
            pltpu.VMEM((GROUPS, LON, LAT), f32),
            dma((PARTS,)), dma((4,)), dma((4,)), dma((2, PARTS, 3)), dma((2, PARTS, 3)),
            dma((2, 3)), dma((2, 3)), dma((3,)), dma((3,)), dma((2,)), dma, dma,
            dma((3,)), dma((4,)),
        ],
        compiler_params=pltpu.CompilerParams(
            collective_id=0, has_side_effects=True, vmem_limit_bytes=56 << 20
        ),
    )(
        spec, sea_mask, cour_lon, wind,
        cour_lat, band_weight, growth_rate, freq_mix, dir_mix, jnp.asarray(fcol), jnp.asarray(dcol),
    )
    step = 88
    whole = pl.BlockSpec(wide, lambda c: (0, 0, 0))
    out = pl.pallas_call(
        finish_kernel,
        out_shape=jax.ShapeDtypeStruct((LON, LOCAL, LAT), f32),
        grid=(pl.cdiv(LOCAL, step),),
        in_specs=[
            smem,
            pl.BlockSpec((LON, step, LAT), lambda c: (0, c, 0)),
            pl.BlockSpec((TILES, step, LAT), lambda c: (0, c, 0)),
            whole, whole, whole,
        ],
        out_specs=pl.BlockSpec((LON, step, LAT), lambda c: (0, c, 0)),
        compiler_params=pltpu.CompilerParams(vmem_limit_bytes=58 << 20),
    )(first, moved, mixed, live, low, place)
    return jnp.transpose(out, (1, 0, 2))


def solution(mesh):
    placed = (
        P("bin", "lon", None),
        P("lon", None),
        P("bin", None),
        P("bin"),
        P("lon", None),
        P(),
        P(),
        P(),
        P(),
        P("lon", None, None),
        P("lon", None),
    )
    return jax.shard_map(
        on_device, mesh=mesh, in_specs=placed, out_specs=P("bin", "lon", None), check_vma=False
    )
```
